256 devices in a mesh: shot: 8 (over x, y_hi), sub: 32 (over y_lo, z, core).
Axes of the slice: x: 4, y: 4 (y_hi: 2, y_lo: 2; y = y_hi * 2 + y_lo), z: 8, core: 2. Of those that a mesh axis runs over, the one named last changes fastest.
Arguments:
- vel_model: bfloat16 [8, 128, 320, 128], P('shot', 'sub'), may hold values from 0.5 to 1
- den_model: bfloat16 [8, 128, 320, 128], P('shot', 'sub'), may hold values from 1 to 4
- cover: int32 [8, 32], replicated, may hold values from 0 to 7
- receivers: int32 [8, 512], P('shot'), may hold values from 0 to 5242879
- observed: float32 [8, 4, 512], P('shot'), may hold values from -6 to 6
- p_now: float32 [8, 128, 320, 128], P('shot', 'sub'), may hold values from -6 to 6
- p_before: float32 [8, 128, 320, 128], P('shot', 'sub'), may hold values from -6 to 6
- q_now: float32 [8, 128, 320, 128], P('shot', 'sub'), may hold values from -6 to 6
- q_before: float32 [8, 128, 320, 128], P('shot', 'sub'), may hold values from -6 to 6
Outputs:
- grad_vel: float32 [8, 128, 320, 128], P('shot', 'sub')
- grad_den: float32 [8, 128, 320, 128], P('shot', 'sub')
The draws below stay inside these ranges and needn't reach their ends.
All inputs are finite; a program needn't handle non-finite values.
Results may differ from the reference program's by a relative error of at most 0.011.
Values may be sent and summed in bfloat16 or wider, within the bound.
A program may use at most 64 MiB of HBM per device.

```python
import math
import jax
import jax.numpy as jnp
from jax import lax

SX = 4
AY = 320
AZ = 128
ITERS = 4
NREC = 512
AX = 128
N_SHOT = 8
N_SUB = 32


def place_ends(drawn, own_key, least, high):
    spot = [jax.random.randint(jax.random.fold_in(own_key, axis), (), 0, length) for axis, length in enumerate(drawn.shape)]
    main_axis = drawn.shape.index(max(drawn.shape))
    beside = spot[:main_axis] + [(spot[main_axis] + 1) % drawn.shape[main_axis]] + spot[main_axis + 1:]
    return drawn.at[tuple(spot)].set(least).at[tuple(beside)].set(high)


def block_scale(key, extent, pieces, low, top_value):
    level, own = 1.0, jax.random.fold_in(key, 6)
    for axis_at, blocks in pieces:
        draws = jnp.exp(jax.random.uniform(jax.random.fold_in(own, axis_at), (blocks,), jnp.float32, low / len(pieces), top_value / len(pieces)))
        level = level * jnp.repeat(draws, extent[axis_at] // blocks).reshape([-1 if axis == axis_at else 1 for axis in range(len(extent))])
    return level


def scatter_about(own_key, dims, scale, limit, split=(), kind=jnp.bfloat16):
    gain = block_scale(own_key, dims, split, -0.22, 0.18) if split else 1.0
    array = jax.random.normal(own_key, dims, jnp.float32) * scale * gain
    return jnp.minimum(jnp.maximum(array, -limit), limit).astype(kind)


def setup_inputs(seed: int = 0) -> dict:
    seeds = jax.random.split(jax.random.key(seed), 10)
    return {
        "vel_model": jnp.clip(0.5 + 0.5 * jax.random.uniform(seeds[0], (N_SHOT, AX, AY, AZ), jnp.float32) ** block_scale(seeds[0], (N_SHOT, AX, AY, AZ), ((0, 8), (1, 32)), -0.2, 0.2), 0.5, 1.0).astype(jnp.bfloat16),
        "den_model": jnp.clip(jnp.exp(math.log(4.0) - 1.3862944 * jax.random.uniform(seeds[1], (N_SHOT, AX, AY, AZ), jnp.float32) ** block_scale(seeds[1], (N_SHOT, AX, AY, AZ), ((0, 8), (1, 32)), -0.2, 0.2)), 1.0, 4.0).astype(jnp.bfloat16),
        "cover": place_ends(jax.random.randint(seeds[2], (N_SHOT, N_SUB), 0, N_SHOT), jax.random.fold_in(seeds[2], 1), 0, N_SHOT - 1).astype(jnp.int32),
        "receivers": place_ends(jax.random.randint(seeds[3], (N_SHOT, NREC), 0, SX * N_SUB * AY * AZ), jax.random.fold_in(seeds[3], 1), 0, (SX * N_SUB * AY * AZ) - 1).astype(jnp.int32),
        "observed": scatter_about(seeds[4], (N_SHOT, ITERS, NREC), 1.0, 6.0, ((0, 8),), jnp.float32),
        "p_now": scatter_about(seeds[5], (N_SHOT, AX, AY, AZ), 1.0, 6.0, ((0, 8), (1, 32)), jnp.float32),
        "p_before": scatter_about(seeds[6], (N_SHOT, AX, AY, AZ), 1.0, 6.0, ((0, 8), (1, 32)), jnp.float32),
        "q_now": scatter_about(seeds[7], (N_SHOT, AX, AY, AZ), 1.0, 6.0, ((0, 8), (1, 32)), jnp.float32),
        "q_before": scatter_about(seeds[8], (N_SHOT, AX, AY, AZ), 1.0, 6.0, ((0, 8), (1, 32)), jnp.float32),
    }


SECOND = (-205.0 / 72.0, 8.0 / 5.0, -1.0 / 5.0, 8.0 / 315.0, -1.0 / 560.0)
FIRST = (4.0 / 5.0, -1.0 / 5.0, 4.0 / 105.0, -1.0 / 280.0)
SPEED = 0.15


def moved(padded, direction, offset):
    window = [slice(4, padded.shape[0] - 4), slice(4, padded.shape[1] - 4), slice(4, padded.shape[2] - 4)]
    window[direction] = slice(4 + offset, padded.shape[direction] - 4 + offset)
    return padded[tuple(window)]


def stencil(padded):
    center = moved(padded, 0, 0)
    laplace = (3.0 * SECOND[0]) * center
    first_diffs = []
    for direction in range(3):
        slope_sum = jnp.zeros_like(center)
        for distance in range(1, 5):
            above_part = moved(padded, direction, distance)
            below_part = moved(padded, direction, -distance)
            laplace = laplace + SECOND[distance] * (above_part + below_part)
            slope_sum = slope_sum + FIRST[distance - 1] * (above_part - below_part)
        first_diffs.append(slope_sum)
    return laplace, first_diffs


def operate(laplace, first_diffs, slopes):
    return laplace - (slopes[0] * first_diffs[0] + slopes[1] * first_diffs[1] + slopes[2] * first_diffs[2])


def reference(vel_model, den_model, cover, receivers, observed, p_now, p_before, q_now, q_before):
    columns = jnp.arange(SX * N_SUB, dtype=jnp.int32)
    grad_vel = jnp.zeros(vel_model.shape, jnp.float32)
    grad_den = jnp.zeros(den_model.shape, jnp.float32)
    for group in range(N_SHOT):
        rows = cover[group][columns // SX].astype(jnp.int32)
        velocity = vel_model[rows, columns].astype(jnp.float32)
        density = den_model[rows, columns].astype(jnp.float32)
        log_den = jnp.log(density)
        unused_lap, slopes = stencil(jnp.pad(log_den, 4))
        scale = SPEED * velocity * velocity
        shape = velocity.shape
        cells = velocity.size
        stations = receivers[group]
        stored = []
        misfits = []
        previous, current = p_before[group], p_now[group]
        for time_step in range(ITERS):
            laplace, diffs = stencil(jnp.pad(current, 4))
            applied = operate(laplace, diffs, slopes)
            stored.append((applied, diffs))
            previous, current = current, 2.0 * current - previous + scale * applied
            misfits.append(current.reshape(-1)[stations] - observed[group, time_step])
        sum_vel = jnp.zeros(shape, jnp.float32)
        sum_den = jnp.zeros(shape, jnp.float32)
        previous, current = q_before[group], q_now[group]
        for time_step in range(ITERS):
            source = jnp.zeros((cells,), jnp.float32).at[stations].add(misfits[ITERS - 1 - time_step]).reshape(shape)
            adjoint = current + source
            laplace, diffs = stencil(jnp.pad(adjoint, 4))
            applied = operate(laplace, diffs, slopes)
            forward_applied, forward_diffs = stored[ITERS - 1 - time_step]
            sum_vel = sum_vel + adjoint * forward_applied
            sum_den = sum_den + (diffs[0] * forward_diffs[0] + diffs[1] * forward_diffs[1] + diffs[2] * forward_diffs[2])
            previous, current = current, 2.0 * adjoint - previous + scale * applied
        shot_vel = ((2.0 * SPEED) * velocity * sum_vel).astype(jnp.bfloat16)
        shot_den = (scale / density * sum_den).astype(jnp.bfloat16)
        grad_vel = grad_vel.at[rows, columns].add(lax.optimization_barrier(shot_vel).astype(jnp.float32))
        grad_den = grad_den.at[rows, columns].add(lax.optimization_barrier(shot_den).astype(jnp.float32))
    return grad_vel, grad_den
```

```python
import functools

import jax
import jax.numpy as jnp
import ml_dtypes
import numpy as np
from jax import lax
from jax.experimental import pallas as pl
from jax.experimental.pallas import tpu as pltpu
from jax.sharding import PartitionSpec as P

MESH = pl.DeviceIdType.MESH
BF16 = jnp.bfloat16
F32 = jnp.float32

ITERS = 4
SECOND = (-205.0 / 72.0, 8.0 / 5.0, -1.0 / 5.0, 8.0 / 315.0, -1.0 / 560.0)
FIRST = (4.0 / 5.0, -1.0 / 5.0, 4.0 / 105.0, -1.0 / 280.0)
SECOND_WHOLE = (8064.0, -1008.0, 128.0, -9.0)
FIRST_WHOLE = (672.0, -168.0, 32.0, -3.0)
SPEED = 0.15

PLANES = 4
ROWS = 64
PAD = 16
WINDOW = ROWS + 2 * PAD
LANES = 128
SUB = 16
LOG = 8
DEN, VEL = 0, 1


def band_y():
    taps = np.zeros((2 * ROWS, 2 * WINDOW), np.float32)
    for row in range(ROWS):
        for m in range(1, 5):
            for base in (0, WINDOW):
                taps[row, base + PAD + row + m] = SECOND_WHOLE[m - 1]
                taps[row, base + PAD + row - m] = SECOND_WHOLE[m - 1]
                taps[ROWS + row, base + PAD + row + m] = FIRST_WHOLE[m - 1]
                taps[ROWS + row, base + PAD + row - m] = -FIRST_WHOLE[m - 1]
    return taps.astype(ml_dtypes.bfloat16)


def band_z():
    taps = np.zeros((2 * LANES, 2 * LANES), np.float32)
    for out in range(LANES):
        for m in range(1, 5):
            for base in (0, LANES):
                if out + m < LANES:
                    taps[base + out + m, out] = SECOND_WHOLE[m - 1]
                    taps[base + out + m, LANES + out] = FIRST_WHOLE[m - 1]
                if out - m >= 0:
                    taps[base + out - m, out] = SECOND_WHOLE[m - 1]
                    taps[base + out - m, LANES + out] = -FIRST_WHOLE[m - 1]
    return taps.astype(ml_dtypes.bfloat16)


def kernel(
    n_shot, n_sub, chunks,
    cover, receivers, observed, taps_y, taps_z,
    vel_hbm, den_hbm, p_now, p_before, q_now, q_before,
    grad_vel, grad_den,
    own_tile, left_tile, right_tile, far_tile, pair_tile, pair_out,
    velocity, density, log_den, slopes, high, low, halo, field, adj,
    kept_l, kept_d, count, source, sum_vel, sum_den, y_part, z_part,
    shot_out, shot_pair, far_out, far_in, right_out, left_out, from_left, from_right,
    load_sem, g_send, g_recv, h_send, h_recv, r_send, r_recv,
):
    s = lax.axis_index("shot")
    c = lax.axis_index("sub")
    right = (lax.rem(s + 2, n_shot), c)
    left = (lax.rem(s + n_shot - 2, n_shot), c)
    y_hi = lax.rem(s, 2)
    pair = (s + 1 - 2 * y_hi, c)
    after = (s, c + 1)
    before = (s, c - 1)
    has_after = c < n_sub - 1
    has_before = c > 0

    loads = [
        pltpu.make_async_copy(den_hbm.at[0], own_tile.at[DEN], load_sem.at[0]),
        pltpu.make_async_copy(vel_hbm.at[0], own_tile.at[VEL], load_sem.at[1]),
        pltpu.make_async_copy(p_now.at[0], field.at[0], load_sem.at[2]),
        pltpu.make_async_copy(p_before.at[0], field.at[1], load_sem.at[3]),
        pltpu.make_async_copy(q_now.at[0], adj.at[0], load_sem.at[4]),
        pltpu.make_async_copy(q_before.at[0], adj.at[1], load_sem.at[5]),
    ]
    for load in loads:
        load.start()

    barrier = pltpu.get_barrier_semaphore()
    for other in (right, left, pair):
        pl.semaphore_signal(barrier, 1, device_id=other, device_id_type=MESH)

    @pl.when(has_after)
    def _():
        pl.semaphore_signal(barrier, 1, device_id=after, device_id_type=MESH)

    @pl.when(has_before)
    def _():
        pl.semaphore_signal(barrier, 1, device_id=before, device_id_type=MESH)

    mine = cover[s, c]
    theirs = cover[pair[0], c]

    def row_of(step):
        return lax.rem(s + 2 * step, n_shot)

    def flag(test):
        return jnp.where(test, 1.0, 0.0).astype(F32)

    steps = (0, 3, 1, 2)
    mine_is = [flag(mine == row_of(k)) for k in steps]
    theirs_is = [flag(theirs == row_of(k)) for k in steps]
    mine_pair = flag(lax.rem(mine, 2) != y_hi)

    def rows(chunk, group=None):
        if group is None:
            return pl.ds(pl.multiple_of(chunk * ROWS, ROWS), ROWS)
        return pl.ds(pl.multiple_of(chunk * ROWS + group * SUB, SUB), SUB)

    def padded(chunk, group=None):
        if group is None:
            return pl.ds(pl.multiple_of(chunk * ROWS + PAD, SUB), ROWS)
        return pl.ds(pl.multiple_of(chunk * ROWS + group * SUB + PAD, SUB), SUB)

    low_half, high_half = pl.ds(0, 2), pl.ds(2, 2)
    every = pl.ds(0, PLANES)

    def g_copy(kind, a, chunk):
        part = rows(chunk)
        if kind == 0:
            src, dst, to = own_tile.at[a, every, part], left_tile.at[a, every, part], right
        elif kind == 1:
            src, dst, to = own_tile.at[a, every, part], right_tile.at[a, every, part], left
        elif kind == 2:
            src, dst, to = left_tile.at[a, low_half, part], far_tile.at[a, low_half, part], right
        elif kind == 3:
            src, dst, to = right_tile.at[a, high_half, part], far_tile.at[a, high_half, part], left
        else:
            src, dst, to = pair_out.at[a, every, part], pair_tile.at[a, every, part], pair
        return pltpu.make_async_remote_copy(
            src_ref=src, dst_ref=dst, send_sem=g_send.at[a, chunk, kind],
            recv_sem=g_recv.at[a, chunk, kind], device_id=to, device_id_type=MESH,
        )

    def h_copy(side, slot, e, chunk):
        return pltpu.make_async_remote_copy(
            src_ref=high.at[slot, every, padded(chunk)],
            dst_ref=halo.at[e, side, every, rows(chunk)],
            send_sem=h_send.at[e, chunk, side], recv_sem=h_recv.at[e, chunk, side],
            device_id=after if side == 0 else before, device_id_type=MESH,
        )

    def h_start(slot, e, chunk):
        @pl.when(has_after)
        def _():
            h_copy(0, slot, e, chunk).start()

        @pl.when(has_before)
        def _():
            h_copy(1, slot, e, chunk).start()

    def h_wait_recv(slot, e, chunk):
        @pl.when(has_before)
        def _():
            h_copy(0, slot, e, chunk).wait_recv()

        @pl.when(has_after)
        def _():
            h_copy(1, slot, e, chunk).wait_recv()

    def h_wait_send(slot, e, chunk):
        @pl.when(has_after)
        def _():
            h_copy(0, slot, e, chunk).wait_send()

        @pl.when(has_before)
        def _():
            h_copy(1, slot, e, chunk).wait_send()

    def r_copy(kind, b, chunk):
        part = rows(chunk)
        if kind == 0:
            src, dst, to = shot_out.at[b, every, part], shot_pair.at[b, every, part], pair
        elif kind == 1:
            src, dst, to = far_out.at[b, low_half, part], far_in.at[b, low_half, part], right
        elif kind == 2:
            src, dst, to = far_out.at[b, high_half, part], far_in.at[b, high_half, part], left
        elif kind == 3:
            src, dst, to = right_out.at[b, every, part], from_left.at[b, every, part], right
        else:
            src, dst, to = left_out.at[b, every, part], from_right.at[b, every, part], left
        return pltpu.make_async_remote_copy(
            src_ref=src, dst_ref=dst, send_sem=r_send.at[b, chunk, kind],
            recv_sem=r_recv.at[b, chunk, kind], device_id=to, device_id_type=MESH,
        )

    def put_split(slot, chunk, group, value):
        top = value.astype(BF16)
        high[slot, :, padded(chunk, group), :] = top
        low[slot, :, padded(chunk, group), :] = (value - top.astype(F32)).astype(BF16)

    def matrix_part(slot, chunk):
        window = pl.ds(pl.multiple_of(chunk * ROWS, ROWS), WINDOW)
        columns = jnp.concatenate(
            [
                jnp.concatenate([ref[slot, plane, window, :] for plane in range(PLANES)], axis=1)
                for ref in (high, low)
            ],
            axis=0,
        )
        y_part[...] = jnp.dot(taps_y[...], columns, preferred_element_type=F32)
        lines = jnp.concatenate(
            [
                jnp.concatenate(
                    [high[slot, plane, padded(chunk), :], low[slot, plane, padded(chunk), :]], axis=1
                )
                for plane in range(PLANES)
            ],
            axis=0,
        )
        z_part[...] = jnp.dot(lines, taps_z[...], preferred_element_type=F32)

    def from_y(group, second):
        part = pl.ds((0 if second else ROWS) + group * SUB, SUB)
        return jnp.stack(
            [y_part[part, pl.ds(plane * LANES, LANES)] for plane in range(PLANES)], axis=0
        )

    def from_z(group, second):
        lanes = pl.ds(0 if second else LANES, LANES)
        return jnp.stack(
            [z_part[pl.ds(plane * ROWS + group * SUB, SUB), lanes] for plane in range(PLANES)],
            axis=0,
        )

    def vector_part(own, e, chunk, group, second):
        wide = jnp.concatenate(
            [
                halo[e, 0, :, rows(chunk, group), :].astype(F32),
                own,
                halo[e, 1, :, rows(chunk, group), :].astype(F32),
            ],
            axis=0,
        )
        d_x = None
        laplace = (3.0 * SECOND[0]) * own if second else None
        for m in range(1, 5):
            up, down = wide[4 + m : 8 + m], wide[4 - m : 8 - m]
            term = FIRST[m - 1] * (up - down)
            d_x = term if d_x is None else d_x + term
            if second:
                laplace = laplace + SECOND[m] * (up + down)
        d_y = from_y(group, False) * (1.0 / 840.0)
        d_z = from_z(group, False) * (1.0 / 840.0)
        if second:
            laplace = laplace + (from_y(group, True) + from_z(group, True)) * (1.0 / 5040.0)
        return laplace, (d_x, d_y, d_z)

    groups = ROWS // SUB

    def operate(laplace, diffs, chunk, group):
        part = rows(chunk, group)
        return laplace - (
            slopes[0, :, part, :] * diffs[0]
            + slopes[1, :, part, :] * diffs[1]
            + slopes[2, :, part, :] * diffs[2]
        )

    def take_tile(a, chunk):
        for kind in (0, 1):
            g_copy(kind, a, chunk).start()

    def relay_tile(a, chunk):
        g_copy(0, a, chunk).wait_recv()
        g_copy(2, a, chunk).start()
        g_copy(1, a, chunk).wait_recv()
        g_copy(3, a, chunk).start()

    def chosen(a, part, flags):
        total = own_tile[a, :, part, :].astype(F32) * flags[0]
        for ref, one in zip((left_tile, right_tile, far_tile), flags[1:]):
            total = total + ref[a, :, part, :].astype(F32) * one
        return total

    def pair_tile_send(a, chunk):
        g_copy(2, a, chunk).wait_recv()
        g_copy(3, a, chunk).wait_recv()
        for group in range(groups):
            part = rows(chunk, group)
            pair_out[a, :, part, :] = chosen(a, part, theirs_is).astype(BF16)
        g_copy(4, a, chunk).start()

    def finish_density(chunk):
        g_copy(4, DEN, chunk).wait_recv()
        for group in range(groups):
            part = rows(chunk, group)
            value = chosen(DEN, part, mine_is) + pair_tile[DEN, :, part, :].astype(F32) * mine_pair
            density[:, part, :] = value
            logs = jnp.log(value)
            log_den[:, part, :] = logs
            put_split(2, chunk, group, logs)
        h_start(2, LOG, chunk)

    def finish_velocity(chunk):
        g_copy(4, VEL, chunk).wait_recv()
        for group in range(groups):
            part = rows(chunk, group)
            velocity[:, part, :] = (
                chosen(VEL, part, mine_is) + pair_tile[VEL, :, part, :].astype(F32) * mine_pair
            )

    def make_slopes(chunk):
        h_wait_recv(2, LOG, chunk)
        matrix_part(2, chunk)
        for group in range(groups):
            part = rows(chunk, group)
            _, diffs = vector_part(log_den[:, part, :], LOG, chunk, group, False)
            for d in range(3):
                slopes[d, :, part, :] = diffs[d]

    def forward(chunk, n):
        now, other = lax.rem(n, 2), lax.rem(n + 1, 2)
        h_wait_recv(now, n, chunk)
        matrix_part(now, chunk)

        @pl.when(n > 0)
        def _():
            h_wait_send(other, n - 1, chunk)

        last = n == ITERS - 1
        for group in range(groups):
            part = rows(chunk, group)
            own = field[now, :, part, :]
            laplace, diffs = vector_part(own, n, chunk, group, True)
            applied = operate(laplace, diffs, chunk, group)
            kept_l[n, :, part, :] = applied
            for d in range(3):
                kept_d[n, d, :, part, :] = diffs[d]
            vel = velocity[:, part, :]
            moved = 2.0 * own - field[other, :, part, :] + (SPEED * vel * vel) * applied
            misfit = count[:, part, :] * moved - source[n, :, part, :]
            source[n, :, part, :] = misfit
            following = jnp.where(last, adj[0, :, part, :] + misfit, moved)
            field[other, :, part, :] = following
            put_split(other, chunk, group, following)
        h_start(other, n + 1, chunk)

    def backward(chunk, n):
        now, other = lax.rem(n, 2), lax.rem(n + 1, 2)
        k = n - ITERS
        h_wait_recv(now, n, chunk)
        matrix_part(now, chunk)
        h_wait_send(other, n - 1, chunk)
        for group in range(groups):
            part = rows(chunk, group)
            own = field[now, :, part, :]
            laplace, diffs = vector_part(own, n, chunk, group, True)
            applied = operate(laplace, diffs, chunk, group)
            vel = velocity[:, part, :]
            moved = 2.0 * own - adj[other, :, part, :] + (SPEED * vel * vel) * applied
            adj[other, :, part, :] = moved
            following = moved + source[2 - k, :, part, :]
            field[other, :, part, :] = following
            put_split(other, chunk, group, following)
            total = sum_vel[:, part, :] + own * kept_l[3 - k, :, part, :]
            sum_vel[:, part, :] = total
            sum_den[:, part, :] += (
                diffs[0] * kept_d[3 - k, 0, :, part, :]
                + diffs[1] * kept_d[3 - k, 1, :, part, :]
                + diffs[2] * kept_d[3 - k, 2, :, part, :]
            )

            @pl.when(k == 2)
            def _():
                whole = total + following * kept_l[0, :, part, :]
                shot_out[VEL, :, part, :] = (2.0 * SPEED * vel * whole).astype(BF16)

        h_start(other, n + 1, chunk)

        @pl.when(k == 2)
        def _():
            r_copy(0, VEL, chunk).start()

    def backward_last(chunk):
        n = 2 * ITERS - 1
        h_wait_recv(n % 2, n, chunk)
        matrix_part(n % 2, chunk)
        for group in range(groups):
            part = rows(chunk, group)
            own = field[n % 2, :, part, :]
            _, diffs = vector_part(own, n, chunk, group, False)
            whole = sum_den[:, part, :] + (
                diffs[0] * kept_d[0, 0, :, part, :]
                + diffs[1] * kept_d[0, 1, :, part, :]
                + diffs[2] * kept_d[0, 2, :, part, :]
            )
            vel = velocity[:, part, :]
            shot_out[DEN, :, part, :] = (
                (SPEED * vel * vel) / density[:, part, :] * whole
            ).astype(BF16)
        r_copy(0, DEN, chunk).start()

    def for_step(b, part, which):
        return (
            shot_out[b, :, part, :].astype(F32) * mine_is[which]
            + shot_pair[b, :, part, :].astype(F32) * theirs_is[which]
        )

    def reduce_far(b, chunk):
        r_copy(0, b, chunk).wait_recv()
        for group in range(groups):
            part = rows(chunk, group)
            far_out[b, :, part, :] = for_step(b, part, 3).astype(BF16)
        r_copy(1, b, chunk).start()
        r_copy(2, b, chunk).start()

    def reduce_near(b, chunk):
        r_copy(1, b, chunk).wait_recv()
        r_copy(2, b, chunk).wait_recv()
        for group in range(groups):
            part = rows(chunk, group)
            arrived = far_in[b, :, part, :].astype(F32)
            to_right = for_step(b, part, 2)
            to_left = for_step(b, part, 1)
            right_out[b, 0:2, part, :] = (to_right[0:2] + arrived[0:2]).astype(BF16)
            right_out[b, 2:4, part, :] = to_right[2:4].astype(BF16)
            left_out[b, 0:2, part, :] = to_left[0:2].astype(BF16)
            left_out[b, 2:4, part, :] = (to_left[2:4] + arrived[2:4]).astype(BF16)
        r_copy(3, b, chunk).start()
        r_copy(4, b, chunk).start()

    def reduce_end(b, chunk):
        r_copy(3, b, chunk).wait_recv()
        r_copy(4, b, chunk).wait_recv()
        out = grad_vel if b == VEL else grad_den
        for group in range(groups):
            part = rows(chunk, group)
            out[0, :, part, :] = (
                for_step(b, part, 0)
                + from_left[b, :, part, :].astype(F32)
                + from_right[b, :, part, :].astype(F32)
            )

    loads[0].wait()
    loads[1].wait()

    barrier_count = 3 + has_after.astype(jnp.int32) + has_before.astype(jnp.int32)
    pl.semaphore_wait(barrier, barrier_count)

    take_tile(DEN, 0)
    take_tile(VEL, 0)

    edge = jnp.zeros((3, PLANES, PAD, LANES), BF16)
    for ref in (high, low):
        ref[:, :, 0:PAD, :] = edge
        ref[:, :, PAD + chunks * ROWS :, :] = edge

    def clear_side(side):
        def clear(i, _):
            halo[i, side] = jnp.zeros((PLANES, chunks * ROWS, LANES), BF16)
            return 0

        lax.fori_loop(0, 9, clear, 0)

    pl.when(c == 0)(lambda: clear_side(0))
    pl.when(c == n_sub - 1)(lambda: clear_side(1))

    loads[2].wait()

    def first_field(chunk, _):
        for group in range(groups):
            put_split(0, chunk, group, field[0, :, rows(chunk, group), :])
        h_start(0, 0, chunk)
        return 0

    lax.fori_loop(0, chunks, first_field, 0)

    place = receivers[...] - c * (PLANES * chunks * ROWS * LANES)
    line = lax.shift_right_arithmetic(place, 7)
    lane = place & (LANES - 1)
    n_rec = receivers.shape[1]
    at_lane = (lax.broadcasted_iota(jnp.int32, (LANES, n_rec), 0) == lane).astype(F32)
    at_lane_16 = at_lane.astype(BF16)
    seen = []
    for n in range(ITERS):
        values = at_lane * observed[0, n : n + 1, :]
        top = values.astype(BF16)
        seen.append(jnp.concatenate([top, (values - top.astype(F32)).astype(BF16)], axis=1))
    contract = (((1,), (1,)), ((), ()))

    def receivers_of_plane(plane, _):
        lines = lax.broadcasted_iota(jnp.int32, (chunks * ROWS, n_rec), 0) + plane * (chunks * ROWS)
        at_line = (lines == line).astype(F32).astype(BF16)
        count[plane] = lax.dot_general(at_line, at_lane_16, contract, preferred_element_type=F32)
        twice = jnp.concatenate([at_line, at_line], axis=1)
        for n in range(ITERS):
            source[n, plane] = lax.dot_general(twice, seen[n], contract, preferred_element_type=F32)
        return 0

    lax.fori_loop(0, PLANES, receivers_of_plane, 0)

    def clear_sums(plane, _):
        sum_vel[plane] = jnp.zeros((chunks * ROWS, LANES), F32)
        sum_den[plane] = jnp.zeros((chunks * ROWS, LANES), F32)
        return 0

    lax.fori_loop(0, PLANES, clear_sums, 0)

    for load in loads[3:]:
        load.wait()

    def at(chunk, event):
        pl.when(jnp.logical_and(chunk >= 0, chunk < chunks))(lambda: event(chunk))

    first_wave = 3
    n_waves = chunks + 2 * ITERS - 1
    ticks = first_wave + n_waves + 4

    def tick(t, _):
        def next_tiles(chunk):
            take_tile(DEN, chunk)
            take_tile(VEL, chunk)

        def relays(chunk):
            relay_tile(DEN, chunk)
            relay_tile(VEL, chunk)

        def pairs(chunk):
            pair_tile_send(DEN, chunk)
            pair_tile_send(VEL, chunk)

        def finish(chunk):
            finish_density(chunk)
            finish_velocity(chunk)

        at(t + 1, next_tiles)
        at(t, relays)
        at(t, pairs)
        at(t - 1, finish)
        wave = t - first_wave
        at(wave, make_slopes)

        def reduce_lag(b, wave_of):
            at(wave - wave_of - 1, functools.partial(reduce_far, b))
            at(wave - wave_of - 2, functools.partial(reduce_near, b))
            at(wave - wave_of - 4, functools.partial(reduce_end, b))

        reduce_lag(VEL, 6)
        reduce_lag(DEN, 7)

        def process(n, _):
            chunk = wave - n
            pl.when(n < ITERS)(lambda: forward(chunk, n))
            pl.when(jnp.logical_and(n >= ITERS, n < 2 * ITERS - 1))(lambda: backward(chunk, n))
            pl.when(n == 2 * ITERS - 1)(lambda: backward_last(chunk))
            return 0

        lax.fori_loop(
            jnp.maximum(wave - (chunks - 1), 0), jnp.minimum(wave + 1, 2 * ITERS), process, 0
        )
        return 0

    lax.fori_loop(0, ticks, tick, 0)

    def drain(chunk, _):
        for a in range(2):
            for kind in range(5):
                g_copy(kind, a, chunk).wait_send()
                r_copy(kind, a, chunk).wait_send()
        h_wait_send(0, 6, chunk)
        h_wait_send(1, 7, chunk)
        h_wait_send(2, LOG, chunk)
        return 0

    lax.fori_loop(0, chunks, drain, 0)


def body(vel_model, den_model, cover, receivers, observed, p_now, p_before, q_now, q_before):
    n_shot, n_sub = lax.axis_size("shot"), lax.axis_size("sub")
    _, planes, length, lanes = vel_model.shape
    chunks = length // ROWS
    tile = (planes, length, lanes)
    tall = (planes, length + 2 * PAD, lanes)
    vmem = pl.BlockSpec(memory_space=pltpu.VMEM)
    anywhere = pl.BlockSpec(memory_space=pl.ANY)
    out = jax.ShapeDtypeStruct((1, *tile), F32)
    return pl.pallas_call(
        functools.partial(kernel, n_shot, n_sub, chunks),
        name="window",
        out_shape=(out, out),
        in_specs=[pl.BlockSpec(memory_space=pltpu.SMEM)] + [vmem] * 4 + [anywhere] * 6,
        out_specs=(vmem, vmem),
        scratch_shapes=[
            *[pltpu.VMEM((2, *tile), BF16) for _ in range(6)],
            pltpu.VMEM(tile, F32),
            pltpu.VMEM(tile, F32),
            pltpu.VMEM(tile, F32),
            pltpu.VMEM((3, *tile), F32),
            pltpu.VMEM((3, *tall), BF16),
            pltpu.VMEM((3, *tall), BF16),
            pltpu.VMEM((9, 2, *tile), BF16),
            pltpu.VMEM((2, *tile), F32),
            pltpu.VMEM((2, *tile), F32),
            pltpu.VMEM((ITERS, *tile), F32),
            pltpu.VMEM((ITERS, 3, *tile), F32),
            pltpu.VMEM(tile, F32),
            pltpu.VMEM((ITERS, *tile), F32),
            pltpu.VMEM(tile, F32),
            pltpu.VMEM(tile, F32),
            pltpu.VMEM((2 * ROWS, PLANES * LANES), F32),
            pltpu.VMEM((PLANES * ROWS, 2 * LANES), F32),
            *[pltpu.VMEM((2, *tile), BF16) for _ in range(8)],
            pltpu.SemaphoreType.DMA((6,)),
            pltpu.SemaphoreType.DMA((2, chunks, 5)),
            pltpu.SemaphoreType.DMA((2, chunks, 5)),
            pltpu.SemaphoreType.DMA((9, chunks, 2)),
            pltpu.SemaphoreType.DMA((9, chunks, 2)),
            pltpu.SemaphoreType.DMA((2, chunks, 5)),
            pltpu.SemaphoreType.DMA((2, chunks, 5)),
        ],
        compiler_params=pltpu.CompilerParams(
            collective_id=0, has_side_effects=True, vmem_limit_bytes=60 * 1024 * 1024
        ),
    )(
        cover, receivers, observed, jnp.asarray(band_y()), jnp.asarray(band_z()),
        vel_model, den_model, p_now, p_before, q_now, q_before,
    )


def solution(mesh):
    tiles = P("shot", "sub", None, None)
    return jax.shard_map(
        body,
        mesh=mesh,
        in_specs=(
            tiles, tiles, P(), P("shot", None), P("shot", None, None), tiles, tiles, tiles, tiles,
        ),
        out_specs=(tiles, tiles),
        check_vma=False,
    )
```

```python
import functools

import jax
import jax.numpy as jnp
import ml_dtypes
import numpy as np
from jax import lax
from jax.experimental import pallas as pl
from jax.experimental.pallas import tpu as pltpu
from jax.sharding import PartitionSpec as P

MESH = pl.DeviceIdType.MESH
BF16 = jnp.bfloat16
F32 = jnp.float32

ITERS = 4
SECOND = (-205.0 / 72.0, 8.0 / 5.0, -1.0 / 5.0, 8.0 / 315.0, -1.0 / 560.0)
FIRST = (4.0 / 5.0, -1.0 / 5.0, 4.0 / 105.0, -1.0 / 280.0)
SECOND_WHOLE = (8064.0, -1008.0, 128.0, -9.0)
FIRST_WHOLE = (672.0, -168.0, 32.0, -3.0)
SPEED = 0.15

PLANES = 4
ROWS = 64
PAD = 16
WINDOW = ROWS + 2 * PAD
LANES = 128
SUB = 16
LOG = 8
DEN, VEL = 0, 1


def band_y():
    taps = np.zeros((2 * ROWS, 2 * WINDOW), np.float32)
    for row in range(ROWS):
        for m in range(1, 5):
            for base in (0, WINDOW):
                taps[row, base + PAD + row + m] = SECOND_WHOLE[m - 1]
                taps[row, base + PAD + row - m] = SECOND_WHOLE[m - 1]
                taps[ROWS + row, base + PAD + row + m] = FIRST_WHOLE[m - 1]
                taps[ROWS + row, base + PAD + row - m] = -FIRST_WHOLE[m - 1]
    return taps.astype(ml_dtypes.bfloat16)


def band_z():
    taps = np.zeros((2 * LANES, 2 * LANES), np.float32)
    for out in range(LANES):
        for m in range(1, 5):
            for base in (0, LANES):
                if out + m < LANES:
                    taps[base + out + m, out] = SECOND_WHOLE[m - 1]
                    taps[base + out + m, LANES + out] = FIRST_WHOLE[m - 1]
                if out - m >= 0:
                    taps[base + out - m, out] = SECOND_WHOLE[m - 1]
                    taps[base + out - m, LANES + out] = -FIRST_WHOLE[m - 1]
    return taps.astype(ml_dtypes.bfloat16)


def kernel(
    n_shot, n_sub, chunks,
    cover, receivers, observed, taps_y, taps_z,
    vel_hbm, den_hbm, p_now, p_before, q_now, q_before,
    grad_vel, grad_den,
    own_tile, left_tile, right_tile, far_tile, pair_tile, pair_out,
    velocity, density, log_den, slopes, high, low, halo, field, adj,
    kept_l, kept_d, count, source, sum_vel, sum_den, y_part, z_part,
    shot_out, shot_pair, far_out, far_in, right_out, left_out, from_left, from_right,
    spot, seen, load_sem, g_send, g_recv, h_send, h_recv, r_send, r_recv,
):
    s = lax.axis_index("shot")
    c = lax.axis_index("sub")
    right = (lax.rem(s + 2, n_shot), c)
    left = (lax.rem(s + n_shot - 2, n_shot), c)
    y_hi = lax.rem(s, 2)
    pair = (s + 1 - 2 * y_hi, c)
    after = (s, c + 1)
    before = (s, c - 1)
    has_after = c < n_sub - 1
    has_before = c > 0

    loads = [
        pltpu.make_async_copy(den_hbm.at[0], own_tile.at[DEN], load_sem.at[0]),
        pltpu.make_async_copy(vel_hbm.at[0], own_tile.at[VEL], load_sem.at[1]),
        pltpu.make_async_copy(p_now.at[0], field.at[0], load_sem.at[2]),
        pltpu.make_async_copy(p_before.at[0], field.at[1], load_sem.at[3]),
        pltpu.make_async_copy(q_now.at[0], adj.at[0], load_sem.at[4]),
        pltpu.make_async_copy(q_before.at[0], adj.at[1], load_sem.at[5]),
    ]
    for load in loads:
        load.start()

    barrier = pltpu.get_barrier_semaphore()
    for other in (right, left, pair):
        pl.semaphore_signal(barrier, 1, device_id=other, device_id_type=MESH)

    @pl.when(has_after)
    def _():
        pl.semaphore_signal(barrier, 1, device_id=after, device_id_type=MESH)

    @pl.when(has_before)
    def _():
        pl.semaphore_signal(barrier, 1, device_id=before, device_id_type=MESH)

    mine = cover[s, c]
    theirs = cover[pair[0], c]

    def row_of(step):
        return lax.rem(s + 2 * step, n_shot)

    def flag(test):
        return jnp.where(test, 1.0, 0.0).astype(F32)

    steps = (0, 3, 1, 2)
    mine_is = [flag(mine == row_of(k)) for k in steps]
    theirs_is = [flag(theirs == row_of(k)) for k in steps]
    mine_pair = flag(lax.rem(mine, 2) != y_hi)

    def rows(chunk, group=None):
        if group is None:
            return pl.ds(pl.multiple_of(chunk * ROWS, ROWS), ROWS)
        return pl.ds(pl.multiple_of(chunk * ROWS + group * SUB, SUB), SUB)

    def padded(chunk, group=None):
        if group is None:
            return pl.ds(pl.multiple_of(chunk * ROWS + PAD, SUB), ROWS)
        return pl.ds(pl.multiple_of(chunk * ROWS + group * SUB + PAD, SUB), SUB)

    low_half, high_half = pl.ds(0, 2), pl.ds(2, 2)
    every = pl.ds(0, PLANES)

    def g_copy(kind, a, chunk):
        part = rows(chunk)
        if kind == 0:
            src, dst, to = own_tile.at[a, every, part], left_tile.at[a, every, part], right
        elif kind == 1:
            src, dst, to = own_tile.at[a, every, part], right_tile.at[a, every, part], left
        elif kind == 2:
            src, dst, to = left_tile.at[a, low_half, part], far_tile.at[a, low_half, part], right
        elif kind == 3:
            src, dst, to = right_tile.at[a, high_half, part], far_tile.at[a, high_half, part], left
        else:
            src, dst, to = pair_out.at[a, every, part], pair_tile.at[a, every, part], pair
        return pltpu.make_async_remote_copy(
            src_ref=src, dst_ref=dst, send_sem=g_send.at[a, chunk, kind],
            recv_sem=g_recv.at[a, chunk, kind], device_id=to, device_id_type=MESH,
        )

    def h_copy(side, slot, e, chunk):
        return pltpu.make_async_remote_copy(
            src_ref=high.at[slot, every, padded(chunk)],
            dst_ref=halo.at[e, side, every, rows(chunk)],
            send_sem=h_send.at[e, chunk, side], recv_sem=h_recv.at[e, chunk, side],
            device_id=after if side == 0 else before, device_id_type=MESH,
        )

    def h_start(slot, e, chunk):
        @pl.when(has_after)
        def _():
            h_copy(0, slot, e, chunk).start()

        @pl.when(has_before)
        def _():
            h_copy(1, slot, e, chunk).start()

    def h_wait_recv(slot, e, chunk):
        @pl.when(has_before)
        def _():
            h_copy(0, slot, e, chunk).wait_recv()

        @pl.when(has_after)
        def _():
            h_copy(1, slot, e, chunk).wait_recv()

    def h_wait_send(slot, e, chunk):
        @pl.when(has_after)
        def _():
            h_copy(0, slot, e, chunk).wait_send()

        @pl.when(has_before)
        def _():
            h_copy(1, slot, e, chunk).wait_send()

    def r_copy(kind, b, chunk):
        part = rows(chunk)
        if kind == 0:
            src, dst, to = shot_out.at[b, every, part], shot_pair.at[b, every, part], pair
        elif kind == 1:
            src, dst, to = far_out.at[b, low_half, part], far_in.at[b, low_half, part], right
        elif kind == 2:
            src, dst, to = far_out.at[b, high_half, part], far_in.at[b, high_half, part], left
        elif kind == 3:
            src, dst, to = right_out.at[b, every, part], from_left.at[b, every, part], right
        else:
            src, dst, to = left_out.at[b, every, part], from_right.at[b, every, part], left
        return pltpu.make_async_remote_copy(
            src_ref=src, dst_ref=dst, send_sem=r_send.at[b, chunk, kind],
            recv_sem=r_recv.at[b, chunk, kind], device_id=to, device_id_type=MESH,
        )

    def put_split(slot, chunk, group, value):
        top = value.astype(BF16)
        high[slot, :, padded(chunk, group), :] = top
        low[slot, :, padded(chunk, group), :] = (value - top.astype(F32)).astype(BF16)

    def matrix_part(slot, chunk):
        window = pl.ds(pl.multiple_of(chunk * ROWS, ROWS), WINDOW)
        columns = jnp.concatenate(
            [
                jnp.concatenate([ref[slot, plane, window, :] for plane in range(PLANES)], axis=1)
                for ref in (high, low)
            ],
            axis=0,
        )
        y_part[...] = jnp.dot(taps_y[...], columns, preferred_element_type=F32)
        lines = jnp.concatenate(
            [
                jnp.concatenate(
                    [high[slot, plane, padded(chunk), :], low[slot, plane, padded(chunk), :]], axis=1
                )
                for plane in range(PLANES)
            ],
            axis=0,
        )
        z_part[...] = jnp.dot(lines, taps_z[...], preferred_element_type=F32)

    def from_y(group, second):
        part = pl.ds((0 if second else ROWS) + group * SUB, SUB)
        return jnp.stack(
            [y_part[part, pl.ds(plane * LANES, LANES)] for plane in range(PLANES)], axis=0
        )

    def from_z(group, second):
        lanes = pl.ds(0 if second else LANES, LANES)
        return jnp.stack(
            [z_part[pl.ds(plane * ROWS + group * SUB, SUB), lanes] for plane in range(PLANES)],
            axis=0,
        )

    def vector_part(own, e, chunk, group, second):
        wide = jnp.concatenate(
            [
                halo[e, 0, :, rows(chunk, group), :].astype(F32),
                own,
                halo[e, 1, :, rows(chunk, group), :].astype(F32),
            ],
            axis=0,
        )
        d_x = None
        laplace = (3.0 * SECOND[0]) * own if second else None
        for m in range(1, 5):
            up, down = wide[4 + m : 8 + m], wide[4 - m : 8 - m]
            term = FIRST[m - 1] * (up - down)
            d_x = term if d_x is None else d_x + term
            if second:
                laplace = laplace + SECOND[m] * (up + down)
        d_y = from_y(group, False) * (1.0 / 840.0)
        d_z = from_z(group, False) * (1.0 / 840.0)
        if second:
            laplace = laplace + (from_y(group, True) + from_z(group, True)) * (1.0 / 5040.0)
        return laplace, (d_x, d_y, d_z)

    groups = ROWS // SUB

    def operate(laplace, diffs, chunk, group):
        part = rows(chunk, group)
        return laplace - (
            slopes[0, :, part, :] * diffs[0]
            + slopes[1, :, part, :] * diffs[1]
            + slopes[2, :, part, :] * diffs[2]
        )

    def take_tile(a, chunk):
        for kind in (0, 1):
            g_copy(kind, a, chunk).start()

    def relay_tile(a, chunk):
        g_copy(0, a, chunk).wait_recv()
        g_copy(2, a, chunk).start()
        g_copy(1, a, chunk).wait_recv()
        g_copy(3, a, chunk).start()

    def chosen(a, part, flags):
        total = own_tile[a, :, part, :].astype(F32) * flags[0]
        for ref, one in zip((left_tile, right_tile, far_tile), flags[1:]):
            total = total + ref[a, :, part, :].astype(F32) * one
        return total

    def pair_tile_send(a, chunk):
        g_copy(2, a, chunk).wait_recv()
        g_copy(3, a, chunk).wait_recv()
        for group in range(groups):
            part = rows(chunk, group)
            pair_out[a, :, part, :] = chosen(a, part, theirs_is).astype(BF16)
        g_copy(4, a, chunk).start()

    def finish_density(chunk):
        g_copy(4, DEN, chunk).wait_recv()
        for group in range(groups):
            part = rows(chunk, group)
            value = chosen(DEN, part, mine_is) + pair_tile[DEN, :, part, :].astype(F32) * mine_pair
            density[:, part, :] = value
            logs = jnp.log(value)
            log_den[:, part, :] = logs
            put_split(2, chunk, group, logs)
        h_start(2, LOG, chunk)

    def finish_velocity(chunk):
        g_copy(4, VEL, chunk).wait_recv()
        for group in range(groups):
            part = rows(chunk, group)
            velocity[:, part, :] = (
                chosen(VEL, part, mine_is) + pair_tile[VEL, :, part, :].astype(F32) * mine_pair
            )

    def make_slopes(chunk):
        h_wait_recv(2, LOG, chunk)
        matrix_part(2, chunk)
        for group in range(groups):
            part = rows(chunk, group)
            _, diffs = vector_part(log_den[:, part, :], LOG, chunk, group, False)
            for d in range(3):
                slopes[d, :, part, :] = diffs[d]

    def forward(chunk, n):
        now, other = lax.rem(n, 2), lax.rem(n + 1, 2)
        h_wait_recv(now, n, chunk)
        matrix_part(now, chunk)

        @pl.when(n > 0)
        def _():
            h_wait_send(other, n - 1, chunk)

        last = n == ITERS - 1
        for group in range(groups):
            part = rows(chunk, group)
            own = field[now, :, part, :]
            laplace, diffs = vector_part(own, n, chunk, group, True)
            applied = operate(laplace, diffs, chunk, group)
            kept_l[n, :, part, :] = applied
            for d in range(3):
                kept_d[n, d, :, part, :] = diffs[d]
            vel = velocity[:, part, :]
            moved = 2.0 * own - field[other, :, part, :] + (SPEED * vel * vel) * applied
            misfit = count[:, part, :] * moved - source[n, :, part, :]
            source[n, :, part, :] = misfit
            following = jnp.where(last, adj[0, :, part, :] + misfit, moved)
            field[other, :, part, :] = following
            put_split(other, chunk, group, following)
        h_start(other, n + 1, chunk)

    def backward(chunk, n):
        now, other = lax.rem(n, 2), lax.rem(n + 1, 2)
        k = n - ITERS
        h_wait_recv(now, n, chunk)
        matrix_part(now, chunk)
        h_wait_send(other, n - 1, chunk)
        for group in range(groups):
            part = rows(chunk, group)
            own = field[now, :, part, :]
            laplace, diffs = vector_part(own, n, chunk, group, True)
            applied = operate(laplace, diffs, chunk, group)
            vel = velocity[:, part, :]
            moved = 2.0 * own - adj[other, :, part, :] + (SPEED * vel * vel) * applied
            adj[other, :, part, :] = moved
            following = moved + source[2 - k, :, part, :]
            field[other, :, part, :] = following
            put_split(other, chunk, group, following)
            total = sum_vel[:, part, :] + own * kept_l[3 - k, :, part, :]
            sum_vel[:, part, :] = total
            sum_den[:, part, :] += (
                diffs[0] * kept_d[3 - k, 0, :, part, :]
                + diffs[1] * kept_d[3 - k, 1, :, part, :]
                + diffs[2] * kept_d[3 - k, 2, :, part, :]
            )

            @pl.when(k == 2)
            def _():
                whole = total + following * kept_l[0, :, part, :]
                shot_out[VEL, :, part, :] = (2.0 * SPEED * vel * whole).astype(BF16)

        h_start(other, n + 1, chunk)

        @pl.when(k == 2)
        def _():
            r_copy(0, VEL, chunk).start()

    def backward_last(chunk):
        n = 2 * ITERS - 1
        h_wait_recv(n % 2, n, chunk)
        matrix_part(n % 2, chunk)
        for group in range(groups):
            part = rows(chunk, group)
            own = field[n % 2, :, part, :]
            _, diffs = vector_part(own, n, chunk, group, False)
            whole = sum_den[:, part, :] + (
                diffs[0] * kept_d[0, 0, :, part, :]
                + diffs[1] * kept_d[0, 1, :, part, :]
                + diffs[2] * kept_d[0, 2, :, part, :]
            )
            vel = velocity[:, part, :]
            shot_out[DEN, :, part, :] = (
                (SPEED * vel * vel) / density[:, part, :] * whole
            ).astype(BF16)
        r_copy(0, DEN, chunk).start()

    def for_step(b, part, which):
        return (
            shot_out[b, :, part, :].astype(F32) * mine_is[which]
            + shot_pair[b, :, part, :].astype(F32) * theirs_is[which]
        )

    def reduce_far(b, chunk):
        r_copy(0, b, chunk).wait_recv()
        for group in range(groups):
            part = rows(chunk, group)
            far_out[b, :, part, :] = for_step(b, part, 3).astype(BF16)
        r_copy(1, b, chunk).start()
        r_copy(2, b, chunk).start()

    def reduce_near(b, chunk):
        r_copy(1, b, chunk).wait_recv()
        r_copy(2, b, chunk).wait_recv()
        for group in range(groups):
            part = rows(chunk, group)
            arrived = far_in[b, :, part, :].astype(F32)
            to_right = for_step(b, part, 2)
            to_left = for_step(b, part, 1)
            right_out[b, 0:2, part, :] = (to_right[0:2] + arrived[0:2]).astype(BF16)
            right_out[b, 2:4, part, :] = to_right[2:4].astype(BF16)
            left_out[b, 0:2, part, :] = to_left[0:2].astype(BF16)
            left_out[b, 2:4, part, :] = (to_left[2:4] + arrived[2:4]).astype(BF16)
        r_copy(3, b, chunk).start()
        r_copy(4, b, chunk).start()

    def reduce_end(b, chunk):
        r_copy(3, b, chunk).wait_recv()
        r_copy(4, b, chunk).wait_recv()
        out = grad_vel if b == VEL else grad_den
        for group in range(groups):
            part = rows(chunk, group)
            out[0, :, part, :] = (
                for_step(b, part, 0)
                + from_left[b, :, part, :].astype(F32)
                + from_right[b, :, part, :].astype(F32)
            )

    loads[0].wait()
    loads[1].wait()

    barrier_count = 3 + has_after.astype(jnp.int32) + has_before.astype(jnp.int32)
    pl.semaphore_wait(barrier, barrier_count)

    for chunk in range(2):
        take_tile(DEN, chunk)
        take_tile(VEL, chunk)

    edge = jnp.zeros((3, PLANES, PAD, LANES), BF16)
    for ref in (high, low):
        ref[:, :, 0:PAD, :] = edge
        ref[:, :, PAD + chunks * ROWS :, :] = edge

    def clear_side(side):
        def clear(i, _):
            halo[i, side] = jnp.zeros((PLANES, chunks * ROWS, LANES), BF16)
            return 0

        lax.fori_loop(0, 9, clear, 0)

    pl.when(c == 0)(lambda: clear_side(0))
    pl.when(c == n_sub - 1)(lambda: clear_side(1))

    loads[2].wait()

    def first_field(chunk, _):
        for group in range(groups):
            put_split(0, chunk, group, field[0, :, rows(chunk, group), :])
        h_start(0, 0, chunk)
        return 0

    lax.fori_loop(0, chunks, first_field, 0)

    cells = PLANES * chunks * ROWS * LANES
    n_rec = receivers.shape[1]

    def receiver_lanes():
        lane = (receivers[...] - c * cells) & (LANES - 1)
        at_lane = (lax.broadcasted_iota(jnp.int32, (LANES, n_rec), 0) == lane).astype(F32)
        spot[...] = at_lane.astype(BF16)
        for n in range(ITERS):
            values = at_lane * observed[0, n : n + 1, :]
            top = values.astype(BF16)
            seen[n, :, 0:n_rec] = top
            seen[n, :, n_rec : 2 * n_rec] = (values - top.astype(F32)).astype(BF16)

    contract = (((1,), (1,)), ((), ()))

    def receivers_of_plane(plane):
        line = lax.shift_right_arithmetic(receivers[...] - c * cells, 7)
        lines = lax.broadcasted_iota(jnp.int32, (chunks * ROWS, n_rec), 0) + plane * (chunks * ROWS)
        at_line = (lines == line).astype(F32).astype(BF16)
        count[plane] = lax.dot_general(at_line, spot[...], contract, preferred_element_type=F32)
        twice = jnp.concatenate([at_line, at_line], axis=1)
        for n in range(ITERS):
            source[n, plane] = lax.dot_general(
                twice, seen[n], contract, preferred_element_type=F32
            )

    def clear_sums(plane, _):
        sum_vel[plane] = jnp.zeros((chunks * ROWS, LANES), F32)
        sum_den[plane] = jnp.zeros((chunks * ROWS, LANES), F32)
        return 0

    lax.fori_loop(0, PLANES, clear_sums, 0)
    receiver_lanes()

    for load in loads[3:]:
        load.wait()

    def at(chunk, event):
        pl.when(jnp.logical_and(chunk >= 0, chunk < chunks))(lambda: event(chunk))

    first_wave = 3
    n_waves = chunks + 2 * ITERS - 1
    ticks = first_wave + n_waves + 4

    def tick(t, _):
        def plane_pair(pair_index):
            receivers_of_plane(2 * pair_index)
            receivers_of_plane(2 * pair_index + 1)

        def next_tiles(chunk):
            take_tile(DEN, chunk)
            take_tile(VEL, chunk)

        def relays(chunk):
            relay_tile(DEN, chunk)
            relay_tile(VEL, chunk)

        def pairs(chunk):
            pair_tile_send(DEN, chunk)
            pair_tile_send(VEL, chunk)

        def finish(chunk):
            finish_density(chunk)
            finish_velocity(chunk)

        at(t, relays)
        at(t + 2, next_tiles)
        at(t - 1, pairs)
        at(t - 2, finish)
        pl.when(t < 2)(lambda: plane_pair(t))
        wave = t - first_wave
        at(wave, make_slopes)

        def reduce_lag(b, wave_of):
            at(wave - wave_of - 1, functools.partial(reduce_far, b))
            at(wave - wave_of - 2, functools.partial(reduce_near, b))
            at(wave - wave_of - 4, functools.partial(reduce_end, b))

        def process(n, _):
            chunk = wave - n
            pl.when(n < ITERS)(lambda: forward(chunk, n))
            pl.when(jnp.logical_and(n >= ITERS, n < 2 * ITERS - 1))(lambda: backward(chunk, n))
            pl.when(n == 2 * ITERS - 1)(lambda: backward_last(chunk))
            return 0

        lax.fori_loop(
            jnp.maximum(wave - (chunks - 1), 0), jnp.minimum(wave + 1, 2 * ITERS), process, 0
        )
        reduce_lag(VEL, 6)
        reduce_lag(DEN, 7)
        return 0

    lax.fori_loop(0, ticks, tick, 0)

    def drain(chunk, _):
        for a in range(2):
            for kind in range(5):
                g_copy(kind, a, chunk).wait_send()
                r_copy(kind, a, chunk).wait_send()
        h_wait_send(0, 6, chunk)
        h_wait_send(1, 7, chunk)
        h_wait_send(2, LOG, chunk)
        return 0

    lax.fori_loop(0, chunks, drain, 0)


def body(vel_model, den_model, cover, receivers, observed, p_now, p_before, q_now, q_before):
    n_shot, n_sub = lax.axis_size("shot"), lax.axis_size("sub")
    _, planes, length, lanes = vel_model.shape
    chunks = length // ROWS
    tile = (planes, length, lanes)
    tall = (planes, length + 2 * PAD, lanes)
    vmem = pl.BlockSpec(memory_space=pltpu.VMEM)
    anywhere = pl.BlockSpec(memory_space=pl.ANY)
    out = jax.ShapeDtypeStruct((1, *tile), F32)
    return pl.pallas_call(
        functools.partial(kernel, n_shot, n_sub, chunks),
        name="window",
        out_shape=(out, out),
        in_specs=[pl.BlockSpec(memory_space=pltpu.SMEM)] + [vmem] * 4 + [anywhere] * 6,
        out_specs=(vmem, vmem),
        scratch_shapes=[
            *[pltpu.VMEM((2, *tile), BF16) for _ in range(6)],
            pltpu.VMEM(tile, F32),
            pltpu.VMEM(tile, F32),
            pltpu.VMEM(tile, F32),
            pltpu.VMEM((3, *tile), F32),
            pltpu.VMEM((3, *tall), BF16),
            pltpu.VMEM((3, *tall), BF16),
            pltpu.VMEM((9, 2, *tile), BF16),
            pltpu.VMEM((2, *tile), F32),
            pltpu.VMEM((2, *tile), F32),
            pltpu.VMEM((ITERS, *tile), F32),
            pltpu.VMEM((ITERS, 3, *tile), F32),
            pltpu.VMEM(tile, F32),
            pltpu.VMEM((ITERS, *tile), F32),
            pltpu.VMEM(tile, F32),
            pltpu.VMEM(tile, F32),
            pltpu.VMEM((2 * ROWS, PLANES * LANES), F32),
            pltpu.VMEM((PLANES * ROWS, 2 * LANES), F32),
            *[pltpu.VMEM((2, *tile), BF16) for _ in range(8)],
            pltpu.VMEM((LANES, receivers.shape[1]), BF16),
            pltpu.VMEM((ITERS, LANES, 2 * receivers.shape[1]), BF16),
            pltpu.SemaphoreType.DMA((6,)),
            pltpu.SemaphoreType.DMA((2, chunks, 5)),
            pltpu.SemaphoreType.DMA((2, chunks, 5)),
            pltpu.SemaphoreType.DMA((9, chunks, 2)),
            pltpu.SemaphoreType.DMA((9, chunks, 2)),
            pltpu.SemaphoreType.DMA((2, chunks, 5)),
            pltpu.SemaphoreType.DMA((2, chunks, 5)),
        ],
        compiler_params=pltpu.CompilerParams(
            collective_id=0, has_side_effects=True, vmem_limit_bytes=60 * 1024 * 1024
        ),
    )(
        cover, receivers, observed, jnp.asarray(band_y()), jnp.asarray(band_z()),
        vel_model, den_model, p_now, p_before, q_now, q_before,
    )


def solution(mesh):
    tiles = P("shot", "sub", None, None)
    return jax.shard_map(
        body,
        mesh=mesh,
        in_specs=(
            tiles, tiles, P(), P("shot", None), P("shot", None, None), tiles, tiles, tiles, tiles,
        ),
        out_specs=(tiles, tiles),
        check_vma=False,
    )
```

```python
import functools

import jax
import jax.numpy as jnp
import ml_dtypes
import numpy as np
from jax import lax
from jax.experimental import pallas as pl
from jax.experimental.pallas import tpu as pltpu
from jax.sharding import PartitionSpec as P

MESH = pl.DeviceIdType.MESH
BF16 = jnp.bfloat16
F32 = jnp.float32

ITERS = 4
SECOND = (-205.0 / 72.0, 8.0 / 5.0, -1.0 / 5.0, 8.0 / 315.0, -1.0 / 560.0)
FIRST = (4.0 / 5.0, -1.0 / 5.0, 4.0 / 105.0, -1.0 / 280.0)
SECOND_WHOLE = (8064.0, -1008.0, 128.0, -9.0)
FIRST_WHOLE = (672.0, -168.0, 32.0, -3.0)
SPEED = 0.15

PLANES = 4
ROWS = 64
PAD = 16
WINDOW = ROWS + 2 * PAD
LANES = 128
SUB = 16
LOG = 8
DEN, VEL = 0, 1


def band_y():
    taps = np.zeros((2 * ROWS, 2 * WINDOW), np.float32)
    for row in range(ROWS):
        for m in range(1, 5):
            for base in (0, WINDOW):
                taps[row, base + PAD + row + m] = SECOND_WHOLE[m - 1]
                taps[row, base + PAD + row - m] = SECOND_WHOLE[m - 1]
                taps[ROWS + row, base + PAD + row + m] = FIRST_WHOLE[m - 1]
                taps[ROWS + row, base + PAD + row - m] = -FIRST_WHOLE[m - 1]
    return taps.astype(ml_dtypes.bfloat16)


def band_z():
    taps = np.zeros((2 * LANES, 2 * LANES), np.float32)
    for out in range(LANES):
        for m in range(1, 5):
            for base in (0, LANES):
                if out + m < LANES:
                    taps[base + out + m, out] = SECOND_WHOLE[m - 1]
                    taps[base + out + m, LANES + out] = FIRST_WHOLE[m - 1]
                if out - m >= 0:
                    taps[base + out - m, out] = SECOND_WHOLE[m - 1]
                    taps[base + out - m, LANES + out] = -FIRST_WHOLE[m - 1]
    return taps.astype(ml_dtypes.bfloat16)


def kernel(
    n_shot, n_sub, chunks,
    cover, receivers, observed, taps_y, taps_z,
    vel_hbm, den_hbm, p_now, p_before, q_now, q_before,
    grad_vel, grad_den,
    own_tile, left_tile, right_tile, far_tile, pair_tile, pair_out,
    velocity, density, log_den, slopes, high, low, halo, field, adj,
    kept_l, kept_d, count, source, sum_vel, sum_den, y_part, z_part,
    shot_out, shot_pair, far_out, far_in, right_out, left_out, near_in,
    spot, seen, load_sem, g_send, g_recv, h_send, h_recv, r_send, r_recv,
):
    s = lax.axis_index("shot")
    c = lax.axis_index("sub")
    right = (lax.rem(s + 2, n_shot), c)
    left = (lax.rem(s + n_shot - 2, n_shot), c)
    y_hi = lax.rem(s, 2)
    pair = (s + 1 - 2 * y_hi, c)
    after = (s, c + 1)
    before = (s, c - 1)
    has_after = c < n_sub - 1
    has_before = c > 0

    loads = [
        pltpu.make_async_copy(den_hbm.at[0], own_tile.at[DEN], load_sem.at[0]),
        pltpu.make_async_copy(vel_hbm.at[0], own_tile.at[VEL], load_sem.at[1]),
        pltpu.make_async_copy(p_now.at[0], field.at[0], load_sem.at[2]),
        pltpu.make_async_copy(p_before.at[0], field.at[1], load_sem.at[3]),
        pltpu.make_async_copy(q_now.at[0], adj.at[0], load_sem.at[4]),
        pltpu.make_async_copy(q_before.at[0], adj.at[1], load_sem.at[5]),
    ]
    for load in loads:
        load.start()

    barrier = pltpu.get_barrier_semaphore()
    for other in (right, left, pair):
        pl.semaphore_signal(barrier, 1, device_id=other, device_id_type=MESH)

    @pl.when(has_after)
    def _():
        pl.semaphore_signal(barrier, 1, device_id=after, device_id_type=MESH)

    @pl.when(has_before)
    def _():
        pl.semaphore_signal(barrier, 1, device_id=before, device_id_type=MESH)

    mine = cover[s, c]
    theirs = cover[pair[0], c]

    def row_of(step):
        return lax.rem(s + 2 * step, n_shot)

    def flag(test):
        return jnp.where(test, 1.0, 0.0).astype(F32)

    steps = (0, 3, 1, 2)
    mine_is = [flag(mine == row_of(k)) for k in steps]
    theirs_is = [flag(theirs == row_of(k)) for k in steps]
    mine_pair = flag(lax.rem(mine, 2) != y_hi)

    def rows(chunk, group=None):
        if group is None:
            return pl.ds(pl.multiple_of(chunk * ROWS, ROWS), ROWS)
        return pl.ds(pl.multiple_of(chunk * ROWS + group * SUB, SUB), SUB)

    def padded(chunk, group=None):
        if group is None:
            return pl.ds(pl.multiple_of(chunk * ROWS + PAD, SUB), ROWS)
        return pl.ds(pl.multiple_of(chunk * ROWS + group * SUB + PAD, SUB), SUB)

    low_half, high_half = pl.ds(0, 2), pl.ds(2, 2)
    every = pl.ds(0, PLANES)

    both = pl.ds(0, 2)

    def remote(src, dst, send, recv, to):
        return pltpu.make_async_remote_copy(
            src_ref=src, dst_ref=dst, send_sem=send, recv_sem=recv, device_id=to, device_id_type=MESH
        )

    def g_copy(kind, chunk):
        part = rows(chunk)
        if kind == 0:
            src, dst, to = own_tile.at[both, every, part], left_tile.at[both, every, part], right
        elif kind == 1:
            src, dst, to = own_tile.at[both, every, part], right_tile.at[both, every, part], left
        elif kind == 2:
            src, dst, to = (
                left_tile.at[both, low_half, part], far_tile.at[both, low_half, part], right
            )
        elif kind == 3:
            src, dst, to = (
                right_tile.at[both, high_half, part], far_tile.at[both, high_half, part], left
            )
        else:
            src, dst, to = pair_out.at[both, every, part], pair_tile.at[both, every, part], pair
        return remote(src, dst, g_send.at[kind], g_recv.at[chunk, (0, 1, 2, 2, 3)[kind]], to)

    def g_wait_far(chunk):
        whole = far_tile.at[both, every, rows(chunk)]
        remote(whole, whole, g_send.at[2], g_recv.at[chunk, 2], right).wait_recv()

    def g_drain():
        for kind in range(5):
            planes = low_half if kind in (2, 3) else every
            whole = far_tile.at[both, planes]
            remote(whole, whole, g_send.at[kind], g_recv.at[0, 0], right).wait_send()

    def h_copy(side, e, chunk):
        return remote(
            high.at[e, every, padded(chunk)], halo.at[e, side, every, rows(chunk)],
            h_send.at[e, side], h_recv.at[e, chunk], after if side == 0 else before,
        )

    def h_start(e, chunk):
        @pl.when(has_after)
        def _():
            h_copy(0, e, chunk).start()

        @pl.when(has_before)
        def _():
            h_copy(1, e, chunk).start()

    inside = jnp.logical_and(has_before, has_after)

    def h_wait_recv(e, chunk):
        @pl.when(inside)
        def _():
            whole = halo.at[e, both, every, rows(chunk)]
            remote(whole, whole, h_send.at[e, 0], h_recv.at[e, chunk], right).wait_recv()

        @pl.when(jnp.logical_not(inside))
        def _():
            one = halo.at[e, 0, every, rows(chunk)]
            remote(one, one, h_send.at[e, 0], h_recv.at[e, chunk], right).wait_recv()

    def h_drain(e, _):
        whole = halo.at[e, 0]

        @pl.when(has_after)
        def _():
            remote(whole, whole, h_send.at[e, 0], h_recv.at[e, 0], right).wait_send()

        @pl.when(has_before)
        def _():
            remote(whole, whole, h_send.at[e, 1], h_recv.at[e, 0], right).wait_send()

        return 0

    def r_copy(kind, b, chunk):
        part = rows(chunk)
        if kind == 0:
            src, dst, to = shot_out.at[b, every, part], shot_pair.at[b, every, part], pair
        elif kind == 1:
            src, dst, to = far_out.at[b, low_half, part], far_in.at[b, low_half, part], right
        elif kind == 2:
            src, dst, to = far_out.at[b, high_half, part], far_in.at[b, high_half, part], left
        elif kind == 3:
            src, dst, to = right_out.at[b, every, part], near_in.at[b, 0, every, part], right
        else:
            src, dst, to = left_out.at[b, every, part], near_in.at[b, 1, every, part], left
        return remote(src, dst, r_send.at[kind], r_recv.at[b, chunk, (0, 1, 1, 2, 2)[kind]], to)

    def r_wait_far(b, chunk):
        whole = far_in.at[b, every, rows(chunk)]
        remote(whole, whole, r_send.at[1], r_recv.at[b, chunk, 1], right).wait_recv()

    def r_wait_near(b, chunk):
        whole = near_in.at[b, both, every, rows(chunk)]
        remote(whole, whole, r_send.at[3], r_recv.at[b, chunk, 2], right).wait_recv()

    def r_drain():
        for kind in range(5):
            planes = low_half if kind in (1, 2) else every
            whole = far_in.at[both, planes]
            remote(whole, whole, r_send.at[kind], r_recv.at[0, 0, 0], right).wait_send()

    def put_split(e, slot, chunk, group, value):
        top = value.astype(BF16)
        high[e, :, padded(chunk, group), :] = top
        low[slot, :, padded(chunk, group), :] = (value - top.astype(F32)).astype(BF16)

    def matrix_part(e, slot, chunk):
        window = pl.ds(pl.multiple_of(chunk * ROWS, ROWS), WINDOW)
        columns = jnp.concatenate(
            [
                jnp.concatenate([ref[at_, plane, window, :] for plane in range(PLANES)], axis=1)
                for ref, at_ in ((high, e), (low, slot))
            ],
            axis=0,
        )
        y_part[...] = jnp.dot(taps_y[...], columns, preferred_element_type=F32)
        lines = jnp.concatenate(
            [
                jnp.concatenate(
                    [high[e, plane, padded(chunk), :], low[slot, plane, padded(chunk), :]], axis=1
                )
                for plane in range(PLANES)
            ],
            axis=0,
        )
        z_part[...] = jnp.dot(lines, taps_z[...], preferred_element_type=F32)

    def from_y(group, second):
        part = pl.ds((0 if second else ROWS) + group * SUB, SUB)
        return jnp.stack(
            [y_part[part, pl.ds(plane * LANES, LANES)] for plane in range(PLANES)], axis=0
        )

    def from_z(group, second):
        lanes = pl.ds(0 if second else LANES, LANES)
        return jnp.stack(
            [z_part[pl.ds(plane * ROWS + group * SUB, SUB), lanes] for plane in range(PLANES)],
            axis=0,
        )

    def vector_part(own, e, chunk, group, second):
        wide = jnp.concatenate(
            [
                halo[e, 0, :, rows(chunk, group), :].astype(F32),
                own,
                halo[e, 1, :, rows(chunk, group), :].astype(F32),
            ],
            axis=0,
        )
        d_x = None
        laplace = (3.0 * SECOND[0]) * own if second else None
        for m in range(1, 5):
            up, down = wide[4 + m : 8 + m], wide[4 - m : 8 - m]
            term = FIRST[m - 1] * (up - down)
            d_x = term if d_x is None else d_x + term
            if second:
                laplace = laplace + SECOND[m] * (up + down)
        d_y = from_y(group, False) * (1.0 / 840.0)
        d_z = from_z(group, False) * (1.0 / 840.0)
        if second:
            laplace = laplace + (from_y(group, True) + from_z(group, True)) * (1.0 / 5040.0)
        return laplace, (d_x, d_y, d_z)

    groups = ROWS // SUB

    def operate(laplace, diffs, chunk, group):
        part = rows(chunk, group)
        return laplace - (
            slopes[0, :, part, :] * diffs[0]
            + slopes[1, :, part, :] * diffs[1]
            + slopes[2, :, part, :] * diffs[2]
        )

    def take_tiles(chunk):
        g_copy(0, chunk).start()
        g_copy(1, chunk).start()

    def relay_tiles(chunk):
        g_copy(0, chunk).wait_recv()
        g_copy(2, chunk).start()
        g_copy(1, chunk).wait_recv()
        g_copy(3, chunk).start()

    def chosen(a, part, flags):
        total = own_tile[a, :, part, :].astype(F32) * flags[0]
        for ref, one in zip((left_tile, right_tile, far_tile), flags[1:]):
            total = total + ref[a, :, part, :].astype(F32) * one
        return total

    def pair_tiles(chunk):
        g_wait_far(chunk)
        for group in range(groups):
            part = rows(chunk, group)
            for a in (DEN, VEL):
                pair_out[a, :, part, :] = chosen(a, part, theirs_is).astype(BF16)
        g_copy(4, chunk).start()

    def finish_density(chunk):
        g_copy(4, chunk).wait_recv()
        for group in range(groups):
            part = rows(chunk, group)
            value = chosen(DEN, part, mine_is) + pair_tile[DEN, :, part, :].astype(F32) * mine_pair
            density[:, part, :] = value
            logs = jnp.log(value)
            log_den[:, part, :] = logs
            put_split(LOG, 2, chunk, group, logs)
        h_start(LOG, chunk)

    def finish_velocity(chunk):
        for group in range(groups):
            part = rows(chunk, group)
            velocity[:, part, :] = (
                chosen(VEL, part, mine_is) + pair_tile[VEL, :, part, :].astype(F32) * mine_pair
            )

    def make_slopes(chunk):
        h_wait_recv(LOG, chunk)
        matrix_part(LOG, 2, chunk)
        for group in range(groups):
            part = rows(chunk, group)
            _, diffs = vector_part(log_den[:, part, :], LOG, chunk, group, False)
            for d in range(3):
                slopes[d, :, part, :] = diffs[d]

    def forward(chunk, n):
        now, other = lax.rem(n, 2), lax.rem(n + 1, 2)
        h_wait_recv(n, chunk)
        matrix_part(n, now, chunk)

        last = n == ITERS - 1
        for group in range(groups):
            part = rows(chunk, group)
            own = field[now, :, part, :]
            laplace, diffs = vector_part(own, n, chunk, group, True)
            applied = operate(laplace, diffs, chunk, group)
            kept_l[n, :, part, :] = applied
            for d in range(3):
                kept_d[n, d, :, part, :] = diffs[d]
            vel = velocity[:, part, :]
            moved = 2.0 * own - field[other, :, part, :] + (SPEED * vel * vel) * applied
            misfit = count[:, part, :] * moved - source[n, :, part, :]
            source[n, :, part, :] = misfit
            following = jnp.where(last, adj[0, :, part, :] + misfit, moved)
            field[other, :, part, :] = following
            put_split(n + 1, other, chunk, group, following)
        h_start(n + 1, chunk)

    def backward(chunk, n):
        now, other = lax.rem(n, 2), lax.rem(n + 1, 2)
        k = n - ITERS
        h_wait_recv(n, chunk)
        matrix_part(n, now, chunk)
        for group in range(groups):
            part = rows(chunk, group)
            own = field[now, :, part, :]
            laplace, diffs = vector_part(own, n, chunk, group, True)
            applied = operate(laplace, diffs, chunk, group)
            vel = velocity[:, part, :]
            moved = 2.0 * own - adj[other, :, part, :] + (SPEED * vel * vel) * applied
            adj[other, :, part, :] = moved
            following = moved + source[2 - k, :, part, :]
            field[other, :, part, :] = following
            put_split(n + 1, other, chunk, group, following)
            total = sum_vel[:, part, :] + own * kept_l[3 - k, :, part, :]
            sum_vel[:, part, :] = total
            sum_den[:, part, :] += (
                diffs[0] * kept_d[3 - k, 0, :, part, :]
                + diffs[1] * kept_d[3 - k, 1, :, part, :]
                + diffs[2] * kept_d[3 - k, 2, :, part, :]
            )

            @pl.when(k == 2)
            def _():
                whole = total + following * kept_l[0, :, part, :]
                shot_out[VEL, :, part, :] = (2.0 * SPEED * vel * whole).astype(BF16)

        h_start(n + 1, chunk)

        @pl.when(k == 2)
        def _():
            r_copy(0, VEL, chunk).start()

    def backward_last(chunk):
        n = 2 * ITERS - 1
        h_wait_recv(n, chunk)
        matrix_part(n, n % 2, chunk)
        for group in range(groups):
            part = rows(chunk, group)
            own = field[n % 2, :, part, :]
            _, diffs = vector_part(own, n, chunk, group, False)
            whole = sum_den[:, part, :] + (
                diffs[0] * kept_d[0, 0, :, part, :]
                + diffs[1] * kept_d[0, 1, :, part, :]
                + diffs[2] * kept_d[0, 2, :, part, :]
            )
            vel = velocity[:, part, :]
            shot_out[DEN, :, part, :] = (
                (SPEED * vel * vel) / density[:, part, :] * whole
            ).astype(BF16)
        r_copy(0, DEN, chunk).start()

    def for_step(b, part, which):
        return (
            shot_out[b, :, part, :].astype(F32) * mine_is[which]
            + shot_pair[b, :, part, :].astype(F32) * theirs_is[which]
        )

    def reduce_far(b, chunk):
        r_copy(0, b, chunk).wait_recv()
        for group in range(groups):
            part = rows(chunk, group)
            far_out[b, :, part, :] = for_step(b, part, 3).astype(BF16)
        r_copy(1, b, chunk).start()
        r_copy(2, b, chunk).start()

    def reduce_near(b, chunk):
        r_wait_far(b, chunk)
        for group in range(groups):
            part = rows(chunk, group)
            arrived = far_in[b, :, part, :].astype(F32)
            to_right = for_step(b, part, 2)
            to_left = for_step(b, part, 1)
            right_out[b, 0:2, part, :] = (to_right[0:2] + arrived[0:2]).astype(BF16)
            right_out[b, 2:4, part, :] = to_right[2:4].astype(BF16)
            left_out[b, 0:2, part, :] = to_left[0:2].astype(BF16)
            left_out[b, 2:4, part, :] = (to_left[2:4] + arrived[2:4]).astype(BF16)
        r_copy(3, b, chunk).start()
        r_copy(4, b, chunk).start()

    def reduce_end(b, chunk):
        r_wait_near(b, chunk)
        out = grad_vel if b == VEL else grad_den
        for group in range(groups):
            part = rows(chunk, group)
            out[0, :, part, :] = (
                for_step(b, part, 0)
                + near_in[b, 0, :, part, :].astype(F32)
                + near_in[b, 1, :, part, :].astype(F32)
            )

    for ref in (high, low):
        edge = jnp.zeros((ref.shape[0], PLANES, PAD, LANES), BF16)
        ref[:, :, 0:PAD, :] = edge
        ref[:, :, PAD + chunks * ROWS :, :] = edge

    def clear_side(side):
        def clear(i, _):
            halo[i, side] = jnp.zeros((PLANES, chunks * ROWS, LANES), BF16)
            return 0

        lax.fori_loop(0, 9, clear, 0)

    pl.when(c == 0)(lambda: clear_side(0))
    pl.when(c == n_sub - 1)(lambda: clear_side(1))

    loads[2].wait()

    def first_field(chunk, _):
        for group in range(groups):
            put_split(0, 0, chunk, group, field[0, :, rows(chunk, group), :])
        return 0

    lax.fori_loop(0, chunks, first_field, 0)

    cells = PLANES * chunks * ROWS * LANES
    n_rec = receivers.shape[1]

    def receiver_lanes():
        lane = (receivers[...] - c * cells) & (LANES - 1)
        at_lane = (lax.broadcasted_iota(jnp.int32, (LANES, n_rec), 0) == lane).astype(F32)
        spot[...] = at_lane.astype(BF16)
        for n in range(ITERS):
            values = at_lane * observed[0, n : n + 1, :]
            top = values.astype(BF16)
            seen[n, :, 0:n_rec] = top
            seen[n, :, n_rec : 2 * n_rec] = (values - top.astype(F32)).astype(BF16)

    contract = (((1,), (1,)), ((), ()))

    def receivers_of_plane(plane):
        line = lax.shift_right_arithmetic(receivers[...] - c * cells, 7)
        lines = lax.broadcasted_iota(jnp.int32, (chunks * ROWS, n_rec), 0) + plane * (chunks * ROWS)
        at_line = (lines == line).astype(F32).astype(BF16)
        count[plane] = lax.dot_general(at_line, spot[...], contract, preferred_element_type=F32)
        twice = jnp.concatenate([at_line, at_line], axis=1)
        for n in range(ITERS):
            source[n, plane] = lax.dot_general(
                twice, seen[n], contract, preferred_element_type=F32
            )

    def clear_sums(plane, _):
        sum_vel[plane] = jnp.zeros((chunks * ROWS, LANES), F32)
        sum_den[plane] = jnp.zeros((chunks * ROWS, LANES), F32)
        return 0

    lax.fori_loop(0, PLANES, clear_sums, 0)
    receiver_lanes()

    loads[0].wait()
    loads[1].wait()
    barrier_count = 3 + has_after.astype(jnp.int32) + has_before.astype(jnp.int32)
    pl.semaphore_wait(barrier, barrier_count)

    for chunk in range(2):
        take_tiles(chunk)

    def first_halo(chunk, _):
        h_start(0, chunk)
        return 0

    lax.fori_loop(0, chunks, first_halo, 0)

    for load in loads[3:]:
        load.wait()

    def at(chunk, event):
        pl.when(jnp.logical_and(chunk >= 0, chunk < chunks))(lambda: event(chunk))

    first_wave = 3
    n_waves = chunks + 2 * ITERS - 1
    ticks = first_wave + n_waves + 4

    def tick(t, _):
        def plane_pair(pair_index):
            receivers_of_plane(2 * pair_index)
            receivers_of_plane(2 * pair_index + 1)

        def finish(chunk):
            finish_density(chunk)
            finish_velocity(chunk)

        at(t, relay_tiles)
        at(t + 2, take_tiles)
        at(t - 1, pair_tiles)
        at(t - 2, finish)
        pl.when(t < 2)(lambda: plane_pair(t))
        wave = t - first_wave
        at(wave, make_slopes)

        def reduce_lag(b, wave_of):
            at(wave - wave_of - 1, functools.partial(reduce_far, b))
            at(wave - wave_of - 2, functools.partial(reduce_near, b))
            at(wave - wave_of - 4, functools.partial(reduce_end, b))

        def process(n, _):
            chunk = wave - n
            pl.when(n < ITERS)(lambda: forward(chunk, n))
            pl.when(jnp.logical_and(n >= ITERS, n < 2 * ITERS - 1))(lambda: backward(chunk, n))
            pl.when(n == 2 * ITERS - 1)(lambda: backward_last(chunk))
            return 0

        lax.fori_loop(
            jnp.maximum(wave - (chunks - 1), 0), jnp.minimum(wave + 1, 2 * ITERS), process, 0
        )
        reduce_lag(VEL, 6)
        reduce_lag(DEN, 7)
        return 0

    lax.fori_loop(0, ticks, tick, 0)

    g_drain()
    lax.fori_loop(0, 9, h_drain, 0)
    r_drain()


def body(vel_model, den_model, cover, receivers, observed, p_now, p_before, q_now, q_before):
    n_shot, n_sub = lax.axis_size("shot"), lax.axis_size("sub")
    _, planes, length, lanes = vel_model.shape
    chunks = length // ROWS
    tile = (planes, length, lanes)
    tall = (planes, length + 2 * PAD, lanes)
    vmem = pl.BlockSpec(memory_space=pltpu.VMEM)
    anywhere = pl.BlockSpec(memory_space=pl.ANY)
    out = jax.ShapeDtypeStruct((1, *tile), F32)
    return pl.pallas_call(
        functools.partial(kernel, n_shot, n_sub, chunks),
        name="window",
        out_shape=(pltpu.VMEM(out.shape, F32), pltpu.VMEM(out.shape, F32)),
        in_specs=[pl.BlockSpec(memory_space=pltpu.SMEM)] + [vmem] * 4 + [anywhere] * 6,
        out_specs=(vmem, vmem),
        scratch_shapes=[
            *[pltpu.VMEM((2, *tile), BF16) for _ in range(6)],
            pltpu.VMEM(tile, F32),
            pltpu.VMEM(tile, F32),
            pltpu.VMEM(tile, F32),
            pltpu.VMEM((3, *tile), F32),
            pltpu.VMEM((9, *tall), BF16),
            pltpu.VMEM((3, *tall), BF16),
            pltpu.VMEM((9, 2, *tile), BF16),
            pltpu.VMEM((2, *tile), F32),
            pltpu.VMEM((2, *tile), F32),
            pltpu.VMEM((ITERS, *tile), F32),
            pltpu.VMEM((ITERS, 3, *tile), F32),
            pltpu.VMEM(tile, F32),
            pltpu.VMEM((ITERS, *tile), F32),
            pltpu.VMEM(tile, F32),
            pltpu.VMEM(tile, F32),
            pltpu.VMEM((2 * ROWS, PLANES * LANES), F32),
            pltpu.VMEM((PLANES * ROWS, 2 * LANES), F32),
            *[pltpu.VMEM((2, *tile), BF16) for _ in range(6)],
            pltpu.VMEM((2, 2, *tile), BF16),
            pltpu.VMEM((LANES, receivers.shape[1]), BF16),
            pltpu.VMEM((ITERS, LANES, 2 * receivers.shape[1]), BF16),
            pltpu.SemaphoreType.DMA((6,)),
            pltpu.SemaphoreType.DMA((5,)),
            pltpu.SemaphoreType.DMA((chunks, 4)),
            pltpu.SemaphoreType.DMA((9, 2)),
            pltpu.SemaphoreType.DMA((9, chunks)),
            pltpu.SemaphoreType.DMA((5,)),
            pltpu.SemaphoreType.DMA((2, chunks, 3)),
        ],
        compiler_params=pltpu.CompilerParams(
            collective_id=0, has_side_effects=True, vmem_limit_bytes=60 * 1024 * 1024
        ),
    )(
        cover, receivers, observed, jnp.asarray(band_y()), jnp.asarray(band_z()),
        vel_model, den_model, p_now, p_before, q_now, q_before,
    )


def solution(mesh):
    tiles = P("shot", "sub", None, None)
    return jax.shard_map(
        body,
        mesh=mesh,
        in_specs=(
            tiles, tiles, P(), P("shot", None), P("shot", None, None), tiles, tiles, tiles, tiles,
        ),
        out_specs=(tiles, tiles),
        check_vma=False,
    )
```

```python
import functools

import jax
import jax.numpy as jnp
import ml_dtypes
import numpy as np
from jax import lax
from jax.experimental import pallas as pl
from jax.experimental.pallas import tpu as pltpu
from jax.sharding import PartitionSpec as P

MESH = pl.DeviceIdType.MESH
BF16 = jnp.bfloat16
F32 = jnp.float32

ITERS = 4
SECOND = (-205.0 / 72.0, 8.0 / 5.0, -1.0 / 5.0, 8.0 / 315.0, -1.0 / 560.0)
FIRST = (4.0 / 5.0, -1.0 / 5.0, 4.0 / 105.0, -1.0 / 280.0)
SECOND_WHOLE = (8064.0, -1008.0, 128.0, -9.0)
FIRST_WHOLE = (672.0, -168.0, 32.0, -3.0)
SPEED = 0.15

PLANES = 4
ROWS = 64
PAD = 16
WINDOW = ROWS + 2 * PAD
LANES = 128
SUB = 16
LOG = 8
DEN, VEL = 0, 1
TILES_DIRECT = 0
SUMS_DIRECT = (1, 0)


def band_y():
    taps = np.zeros((2 * ROWS, 2 * WINDOW), np.float32)
    for row in range(ROWS):
        for m in range(1, 5):
            for base in (0, WINDOW):
                taps[row, base + PAD + row + m] = SECOND_WHOLE[m - 1]
                taps[row, base + PAD + row - m] = SECOND_WHOLE[m - 1]
                taps[ROWS + row, base + PAD + row + m] = FIRST_WHOLE[m - 1]
                taps[ROWS + row, base + PAD + row - m] = -FIRST_WHOLE[m - 1]
    return taps.astype(ml_dtypes.bfloat16)


def band_z():
    taps = np.zeros((2 * LANES, 2 * LANES), np.float32)
    for out in range(LANES):
        for m in range(1, 5):
            for base in (0, LANES):
                if out + m < LANES:
                    taps[base + out + m, out] = SECOND_WHOLE[m - 1]
                    taps[base + out + m, LANES + out] = FIRST_WHOLE[m - 1]
                if out - m >= 0:
                    taps[base + out - m, out] = SECOND_WHOLE[m - 1]
                    taps[base + out - m, LANES + out] = -FIRST_WHOLE[m - 1]
    return taps.astype(ml_dtypes.bfloat16)


def kernel(
    n_shot, n_sub, chunks,
    cover, receivers, observed, taps_y, taps_z,
    vel_hbm, den_hbm, p_now, p_before, q_now, q_before,
    grad_vel, grad_den,
    own_tile, left_tile, right_tile, far_tile, pair_tile, pair_out,
    velocity, density, log_den, slopes, high, low, halo, field, adj,
    kept_l, kept_d, count, source, sum_vel, sum_den, y_part, z_part,
    shot_out, shot_pair, far_out, far_in, right_out, left_out, near_in,
    spot, seen, load_sem, g_send, g_recv, h_send, h_recv, r_send, r_recv,
):
    s = lax.axis_index("shot")
    c = lax.axis_index("sub")
    right = (lax.rem(s + 2, n_shot), c)
    left = (lax.rem(s + n_shot - 2, n_shot), c)
    far = (lax.rem(s + 4, n_shot), c)
    y_hi = lax.rem(s, 2)
    pair = (s + 1 - 2 * y_hi, c)
    after = (s, c + 1)
    before = (s, c - 1)
    has_after = c < n_sub - 1
    has_before = c > 0

    loads = [
        pltpu.make_async_copy(den_hbm.at[0], own_tile.at[DEN], load_sem.at[0]),
        pltpu.make_async_copy(vel_hbm.at[0], own_tile.at[VEL], load_sem.at[1]),
        pltpu.make_async_copy(p_now.at[0], field.at[0], load_sem.at[2]),
        pltpu.make_async_copy(p_before.at[0], field.at[1], load_sem.at[3]),
        pltpu.make_async_copy(q_now.at[0], adj.at[0], load_sem.at[4]),
        pltpu.make_async_copy(q_before.at[0], adj.at[1], load_sem.at[5]),
    ]
    for load in loads:
        load.start()

    barrier = pltpu.get_barrier_semaphore()
    for other in (right, left, far, pair):
        pl.semaphore_signal(barrier, 1, device_id=other, device_id_type=MESH)

    @pl.when(has_after)
    def _():
        pl.semaphore_signal(barrier, 1, device_id=after, device_id_type=MESH)

    @pl.when(has_before)
    def _():
        pl.semaphore_signal(barrier, 1, device_id=before, device_id_type=MESH)

    mine = cover[s, c]
    theirs = cover[pair[0], c]

    def row_of(step):
        return lax.rem(s + 2 * step, n_shot)

    def flag(test):
        return jnp.where(test, 1.0, 0.0).astype(F32)

    steps = (0, 3, 1, 2)
    mine_is = [flag(mine == row_of(k)) for k in steps]
    theirs_is = [flag(theirs == row_of(k)) for k in steps]
    mine_pair = flag(lax.rem(mine, 2) != y_hi)

    def rows(chunk, group=None):
        if group is None:
            return pl.ds(pl.multiple_of(chunk * ROWS, ROWS), ROWS)
        return pl.ds(pl.multiple_of(chunk * ROWS + group * SUB, SUB), SUB)

    def padded(chunk, group=None):
        if group is None:
            return pl.ds(pl.multiple_of(chunk * ROWS + PAD, SUB), ROWS)
        return pl.ds(pl.multiple_of(chunk * ROWS + group * SUB + PAD, SUB), SUB)

    low_half, high_half = pl.ds(0, 2), pl.ds(2, 2)
    every = pl.ds(0, PLANES)

    both = pl.ds(0, 2)
    tiles_relayed = chunks - TILES_DIRECT
    sums_relayed = (chunks - SUMS_DIRECT[DEN], chunks - SUMS_DIRECT[VEL])

    def remote(src, dst, send, recv, to):
        return pltpu.make_async_remote_copy(
            src_ref=src, dst_ref=dst, send_sem=send, recv_sem=recv, device_id=to, device_id_type=MESH
        )

    def g_copy(kind, chunk):
        part = rows(chunk)
        if kind == 0:
            src, dst, to = own_tile.at[both, every, part], left_tile.at[both, every, part], right
        elif kind == 1:
            src, dst, to = own_tile.at[both, every, part], right_tile.at[both, every, part], left
        elif kind == 2:
            src, dst, to = (
                left_tile.at[both, low_half, part], far_tile.at[both, low_half, part], right
            )
        elif kind == 3:
            src, dst, to = (
                right_tile.at[both, high_half, part], far_tile.at[both, high_half, part], left
            )
        elif kind == 4:
            src, dst, to = pair_out.at[both, every, part], pair_tile.at[both, every, part], pair
        else:
            src, dst, to = own_tile.at[both, every, part], far_tile.at[both, every, part], far
        return remote(src, dst, g_send.at[kind], g_recv.at[chunk, (0, 1, 2, 2, 3, 2)[kind]], to)

    def g_wait_far(chunk):
        whole = far_tile.at[both, every, rows(chunk)]
        remote(whole, whole, g_send.at[2], g_recv.at[chunk, 2], right).wait_recv()

    def g_drain():
        for kind in range(6):
            planes = low_half if kind in (2, 3) else every
            sent = {2: tiles_relayed, 3: tiles_relayed, 5: chunks - tiles_relayed}.get(kind, chunks)
            if sent:
                whole = far_tile.at[both, planes, pl.ds(0, sent * ROWS)]
                remote(whole, whole, g_send.at[kind], g_recv.at[0, 0], right).wait_send()

    def h_copy(side, e, chunk):
        return remote(
            high.at[e, every, padded(chunk)], halo.at[e, side, every, rows(chunk)],
            h_send.at[e, side], h_recv.at[e, chunk], after if side == 0 else before,
        )

    def h_start(e, chunk):
        @pl.when(has_after)
        def _():
            h_copy(0, e, chunk).start()

        @pl.when(has_before)
        def _():
            h_copy(1, e, chunk).start()

    inside = jnp.logical_and(has_before, has_after)

    def h_wait_recv(e, chunk):
        @pl.when(inside)
        def _():
            whole = halo.at[e, both, every, rows(chunk)]
            remote(whole, whole, h_send.at[e, 0], h_recv.at[e, chunk], right).wait_recv()

        @pl.when(jnp.logical_not(inside))
        def _():
            one = halo.at[e, 0, every, rows(chunk)]
            remote(one, one, h_send.at[e, 0], h_recv.at[e, chunk], right).wait_recv()

    def h_drain(e, _):
        whole = halo.at[e, 0]

        @pl.when(has_after)
        def _():
            remote(whole, whole, h_send.at[e, 0], h_recv.at[e, 0], right).wait_send()

        @pl.when(has_before)
        def _():
            remote(whole, whole, h_send.at[e, 1], h_recv.at[e, 0], right).wait_send()

        return 0

    def r_copy(kind, b, chunk):
        part = rows(chunk)
        if kind == 0:
            src, dst, to = shot_out.at[b, every, part], shot_pair.at[b, every, part], pair
        elif kind == 1:
            src, dst, to = far_out.at[b, low_half, part], far_in.at[b, low_half, part], right
        elif kind == 2:
            src, dst, to = far_out.at[b, high_half, part], far_in.at[b, high_half, part], left
        elif kind == 3:
            src, dst, to = right_out.at[b, every, part], near_in.at[b, 0, every, part], right
        elif kind == 4:
            src, dst, to = left_out.at[b, every, part], near_in.at[b, 1, every, part], left
        else:
            src, dst, to = far_out.at[b, every, part], far_in.at[b, every, part], far
        return remote(
            src, dst, r_send.at[b, kind], r_recv.at[b, chunk, (0, 1, 1, 2, 2, 1)[kind]], to
        )

    def r_wait_far(b, chunk):
        whole = far_in.at[b, every, rows(chunk)]
        remote(whole, whole, r_send.at[b, 1], r_recv.at[b, chunk, 1], right).wait_recv()

    def r_wait_near(b, chunk):
        whole = near_in.at[b, both, every, rows(chunk)]
        remote(whole, whole, r_send.at[b, 3], r_recv.at[b, chunk, 2], right).wait_recv()

    def r_drain():
        for b in (DEN, VEL):
            for kind in range(6):
                planes = low_half if kind in (1, 2) else every
                relayed = sums_relayed[b]
                sent = {1: relayed, 2: relayed, 5: chunks - relayed}.get(kind, chunks)
                if sent:
                    whole = far_in.at[b, planes, pl.ds(0, sent * ROWS)]
                    remote(whole, whole, r_send.at[b, kind], r_recv.at[0, 0, 0], right).wait_send()

    def put_split(e, slot, chunk, group, value):
        top = value.astype(BF16)
        high[e, :, padded(chunk, group), :] = top
        low[slot, :, padded(chunk, group), :] = (value - top.astype(F32)).astype(BF16)

    def matrix_part(e, slot, chunk):
        window = pl.ds(pl.multiple_of(chunk * ROWS, ROWS), WINDOW)
        columns = jnp.concatenate(
            [
                jnp.concatenate([ref[at_, plane, window, :] for plane in range(PLANES)], axis=1)
                for ref, at_ in ((high, e), (low, slot))
            ],
            axis=0,
        )
        y_part[...] = jnp.dot(taps_y[...], columns, preferred_element_type=F32)
        lines = jnp.concatenate(
            [
                jnp.concatenate(
                    [high[e, plane, padded(chunk), :], low[slot, plane, padded(chunk), :]], axis=1
                )
                for plane in range(PLANES)
            ],
            axis=0,
        )
        z_part[...] = jnp.dot(lines, taps_z[...], preferred_element_type=F32)

    def from_y(group, second):
        part = pl.ds((0 if second else ROWS) + group * SUB, SUB)
        return jnp.stack(
            [y_part[part, pl.ds(plane * LANES, LANES)] for plane in range(PLANES)], axis=0
        )

    def from_z(group, second):
        lanes = pl.ds(0 if second else LANES, LANES)
        return jnp.stack(
            [z_part[pl.ds(plane * ROWS + group * SUB, SUB), lanes] for plane in range(PLANES)],
            axis=0,
        )

    def vector_part(own, e, chunk, group, second):
        wide = jnp.concatenate(
            [
                halo[e, 0, :, rows(chunk, group), :].astype(F32),
                own,
                halo[e, 1, :, rows(chunk, group), :].astype(F32),
            ],
            axis=0,
        )
        d_x = None
        laplace = (3.0 * SECOND[0]) * own if second else None
        for m in range(1, 5):
            up, down = wide[4 + m : 8 + m], wide[4 - m : 8 - m]
            term = FIRST[m - 1] * (up - down)
            d_x = term if d_x is None else d_x + term
            if second:
                laplace = laplace + SECOND[m] * (up + down)
        d_y = from_y(group, False) * (1.0 / 840.0)
        d_z = from_z(group, False) * (1.0 / 840.0)
        if second:
            laplace = laplace + (from_y(group, True) + from_z(group, True)) * (1.0 / 5040.0)
        return laplace, (d_x, d_y, d_z)

    groups = ROWS // SUB

    def operate(laplace, diffs, chunk, group):
        part = rows(chunk, group)
        return laplace - (
            slopes[0, :, part, :] * diffs[0]
            + slopes[1, :, part, :] * diffs[1]
            + slopes[2, :, part, :] * diffs[2]
        )

    def take_tiles(chunk):
        g_copy(0, chunk).start()
        g_copy(1, chunk).start()
        pl.when(chunk >= tiles_relayed)(lambda: g_copy(5, chunk).start())

    def relay_tiles(chunk):
        g_copy(0, chunk).wait_recv()
        pl.when(chunk < tiles_relayed)(lambda: g_copy(2, chunk).start())
        g_copy(1, chunk).wait_recv()
        pl.when(chunk < tiles_relayed)(lambda: g_copy(3, chunk).start())

    def chosen(a, part, flags):
        total = own_tile[a, :, part, :].astype(F32) * flags[0]
        for ref, one in zip((left_tile, right_tile, far_tile), flags[1:]):
            total = total + ref[a, :, part, :].astype(F32) * one
        return total

    def pair_tiles(chunk):
        g_wait_far(chunk)
        for group in range(groups):
            part = rows(chunk, group)
            for a in (DEN, VEL):
                pair_out[a, :, part, :] = chosen(a, part, theirs_is).astype(BF16)
        g_copy(4, chunk).start()

    def finish_density(chunk):
        g_copy(4, chunk).wait_recv()
        for group in range(groups):
            part = rows(chunk, group)
            value = chosen(DEN, part, mine_is) + pair_tile[DEN, :, part, :].astype(F32) * mine_pair
            density[:, part, :] = value
            logs = jnp.log(value)
            log_den[:, part, :] = logs
            put_split(LOG, 2, chunk, group, logs)
        h_start(LOG, chunk)

    def finish_velocity(chunk):
        for group in range(groups):
            part = rows(chunk, group)
            velocity[:, part, :] = (
                chosen(VEL, part, mine_is) + pair_tile[VEL, :, part, :].astype(F32) * mine_pair
            )

    def make_slopes(chunk):
        h_wait_recv(LOG, chunk)
        matrix_part(LOG, 2, chunk)
        for group in range(groups):
            part = rows(chunk, group)
            _, diffs = vector_part(log_den[:, part, :], LOG, chunk, group, False)
            for d in range(3):
                slopes[d, :, part, :] = diffs[d]

    def forward(chunk, n):
        now, other = lax.rem(n, 2), lax.rem(n + 1, 2)
        h_wait_recv(n, chunk)
        matrix_part(n, now, chunk)

        last = n == ITERS - 1
        for group in range(groups):
            part = rows(chunk, group)
            own = field[now, :, part, :]
            laplace, diffs = vector_part(own, n, chunk, group, True)
            applied = operate(laplace, diffs, chunk, group)
            kept_l[n, :, part, :] = applied
            for d in range(3):
                kept_d[n, d, :, part, :] = diffs[d]
            vel = velocity[:, part, :]
            moved = 2.0 * own - field[other, :, part, :] + (SPEED * vel * vel) * applied
            misfit = count[:, part, :] * moved - source[n, :, part, :]
            source[n, :, part, :] = misfit
            following = jnp.where(last, adj[0, :, part, :] + misfit, moved)
            field[other, :, part, :] = following
            put_split(n + 1, other, chunk, group, following)
        h_start(n + 1, chunk)

    def backward(chunk, n):
        now, other = lax.rem(n, 2), lax.rem(n + 1, 2)
        k = n - ITERS
        h_wait_recv(n, chunk)
        matrix_part(n, now, chunk)
        for group in range(groups):
            part = rows(chunk, group)
            own = field[now, :, part, :]
            laplace, diffs = vector_part(own, n, chunk, group, True)
            applied = operate(laplace, diffs, chunk, group)
            vel = velocity[:, part, :]
            moved = 2.0 * own - adj[other, :, part, :] + (SPEED * vel * vel) * applied
            adj[other, :, part, :] = moved
            following = moved + source[2 - k, :, part, :]
            field[other, :, part, :] = following
            put_split(n + 1, other, chunk, group, following)
            total = sum_vel[:, part, :] + own * kept_l[3 - k, :, part, :]
            sum_vel[:, part, :] = total
            sum_den[:, part, :] += (
                diffs[0] * kept_d[3 - k, 0, :, part, :]
                + diffs[1] * kept_d[3 - k, 1, :, part, :]
                + diffs[2] * kept_d[3 - k, 2, :, part, :]
            )

            @pl.when(k == 2)
            def _():
                whole = total + following * kept_l[0, :, part, :]
                shot_out[VEL, :, part, :] = (2.0 * SPEED * vel * whole).astype(BF16)

        h_start(n + 1, chunk)

        @pl.when(k == 2)
        def _():
            r_copy(0, VEL, chunk).start()

    def backward_last(chunk):
        n = 2 * ITERS - 1
        h_wait_recv(n, chunk)
        matrix_part(n, n % 2, chunk)
        for group in range(groups):
            part = rows(chunk, group)
            own = field[n % 2, :, part, :]
            _, diffs = vector_part(own, n, chunk, group, False)
            whole = sum_den[:, part, :] + (
                diffs[0] * kept_d[0, 0, :, part, :]
                + diffs[1] * kept_d[0, 1, :, part, :]
                + diffs[2] * kept_d[0, 2, :, part, :]
            )
            vel = velocity[:, part, :]
            shot_out[DEN, :, part, :] = (
                (SPEED * vel * vel) / density[:, part, :] * whole
            ).astype(BF16)
        r_copy(0, DEN, chunk).start()

    def for_step(b, part, which):
        return (
            shot_out[b, :, part, :].astype(F32) * mine_is[which]
            + shot_pair[b, :, part, :].astype(F32) * theirs_is[which]
        )

    def reduce_far(b, chunk):
        r_copy(0, b, chunk).wait_recv()
        straight = chunk >= sums_relayed[b]
        for group in range(groups):
            part = rows(chunk, group)
            far_out[b, :, part, :] = for_step(b, part, 3).astype(BF16)

        @pl.when(straight)
        def _():
            r_copy(5, b, chunk).start()
            for group in range(groups):
                part = rows(chunk, group)
                right_out[b, :, part, :] = for_step(b, part, 2).astype(BF16)
                left_out[b, :, part, :] = for_step(b, part, 1).astype(BF16)
            r_copy(3, b, chunk).start()
            r_copy(4, b, chunk).start()

        @pl.when(jnp.logical_not(straight))
        def _():
            r_copy(1, b, chunk).start()
            r_copy(2, b, chunk).start()

    def reduce_near(b, chunk):
        @pl.when(chunk < sums_relayed[b])
        def _():
            r_wait_far(b, chunk)
            for group in range(groups):
                part = rows(chunk, group)
                arrived = far_in[b, :, part, :].astype(F32)
                to_right = for_step(b, part, 2)
                to_left = for_step(b, part, 1)
                right_out[b, 0:2, part, :] = (to_right[0:2] + arrived[0:2]).astype(BF16)
                right_out[b, 2:4, part, :] = to_right[2:4].astype(BF16)
                left_out[b, 0:2, part, :] = to_left[0:2].astype(BF16)
                left_out[b, 2:4, part, :] = (to_left[2:4] + arrived[2:4]).astype(BF16)
            r_copy(3, b, chunk).start()
            r_copy(4, b, chunk).start()

    def reduce_end(b, chunk):
        r_wait_near(b, chunk)
        out = grad_vel if b == VEL else grad_den
        for group in range(groups):
            part = rows(chunk, group)
            out[0, :, part, :] = (
                for_step(b, part, 0)
                + near_in[b, 0, :, part, :].astype(F32)
                + near_in[b, 1, :, part, :].astype(F32)
            )

        @pl.when(chunk >= sums_relayed[b])
        def _():
            r_wait_far(b, chunk)
            for group in range(groups):
                part = rows(chunk, group)
                out[0, :, part, :] += far_in[b, :, part, :].astype(F32)

    for ref in (high, low):
        edge = jnp.zeros((ref.shape[0], PLANES, PAD, LANES), BF16)
        ref[:, :, 0:PAD, :] = edge
        ref[:, :, PAD + chunks * ROWS :, :] = edge

    def clear_side(side):
        def clear(i, _):
            halo[i, side] = jnp.zeros((PLANES, chunks * ROWS, LANES), BF16)
            return 0

        lax.fori_loop(0, 9, clear, 0)

    pl.when(c == 0)(lambda: clear_side(0))
    pl.when(c == n_sub - 1)(lambda: clear_side(1))

    loads[2].wait()

    def first_field(chunk, _):
        for group in range(groups):
            put_split(0, 0, chunk, group, field[0, :, rows(chunk, group), :])
        return 0

    lax.fori_loop(0, chunks, first_field, 0)

    cells = PLANES * chunks * ROWS * LANES
    n_rec = receivers.shape[1]

    def receiver_lanes():
        lane = (receivers[...] - c * cells) & (LANES - 1)
        at_lane = (lax.broadcasted_iota(jnp.int32, (LANES, n_rec), 0) == lane).astype(F32)
        spot[...] = at_lane.astype(BF16)
        for n in range(ITERS):
            values = at_lane * observed[0, n : n + 1, :]
            top = values.astype(BF16)
            seen[n, :, 0:n_rec] = top
            seen[n, :, n_rec : 2 * n_rec] = (values - top.astype(F32)).astype(BF16)

    contract = (((1,), (1,)), ((), ()))

    def receivers_of_plane(plane):
        line = lax.shift_right_arithmetic(receivers[...] - c * cells, 7)
        lines = lax.broadcasted_iota(jnp.int32, (chunks * ROWS, n_rec), 0) + plane * (chunks * ROWS)
        at_line = (lines == line).astype(F32).astype(BF16)
        count[plane] = lax.dot_general(at_line, spot[...], contract, preferred_element_type=F32)
        twice = jnp.concatenate([at_line, at_line], axis=1)
        for n in range(ITERS):
            source[n, plane] = lax.dot_general(
                twice, seen[n], contract, preferred_element_type=F32
            )

    def clear_sums(plane, _):
        sum_vel[plane] = jnp.zeros((chunks * ROWS, LANES), F32)
        sum_den[plane] = jnp.zeros((chunks * ROWS, LANES), F32)
        return 0

    lax.fori_loop(0, PLANES, clear_sums, 0)
    receiver_lanes()

    loads[0].wait()
    loads[1].wait()
    barrier_count = 4 + has_after.astype(jnp.int32) + has_before.astype(jnp.int32)
    pl.semaphore_wait(barrier, barrier_count)

    for chunk in range(2):
        take_tiles(chunk)

    def first_halo(chunk, _):
        h_start(0, chunk)
        return 0

    lax.fori_loop(0, chunks, first_halo, 0)

    for load in loads[3:]:
        load.wait()

    def at(chunk, event):
        pl.when(jnp.logical_and(chunk >= 0, chunk < chunks))(lambda: event(chunk))

    first_wave = 3
    n_waves = chunks + 2 * ITERS - 1
    ticks = first_wave + n_waves + 4

    def tick(t, _):
        def plane_pair(pair_index):
            receivers_of_plane(2 * pair_index)
            receivers_of_plane(2 * pair_index + 1)

        def finish(chunk):
            finish_density(chunk)
            finish_velocity(chunk)

        at(t, relay_tiles)
        at(t + 2, take_tiles)
        at(t - 1, pair_tiles)
        at(t - 2, finish)
        pl.when(t < 2)(lambda: plane_pair(t))
        wave = t - first_wave
        at(wave, make_slopes)

        def reduce_lag(b, wave_of):
            at(wave - wave_of - 1, functools.partial(reduce_far, b))
            at(wave - wave_of - 2, functools.partial(reduce_near, b))
            at(wave - wave_of - 4, functools.partial(reduce_end, b))

        def process(n, _):
            chunk = wave - n
            pl.when(n < ITERS)(lambda: forward(chunk, n))
            pl.when(jnp.logical_and(n >= ITERS, n < 2 * ITERS - 1))(lambda: backward(chunk, n))
            pl.when(n == 2 * ITERS - 1)(lambda: backward_last(chunk))
            return 0

        lax.fori_loop(
            jnp.maximum(wave - (chunks - 1), 0), jnp.minimum(wave + 1, 2 * ITERS), process, 0
        )
        reduce_lag(VEL, 6)
        reduce_lag(DEN, 7)
        return 0

    lax.fori_loop(0, ticks, tick, 0)

    g_drain()
    lax.fori_loop(0, 9, h_drain, 0)
    r_drain()


def body(vel_model, den_model, cover, receivers, observed, p_now, p_before, q_now, q_before):
    n_shot, n_sub = lax.axis_size("shot"), lax.axis_size("sub")
    _, planes, length, lanes = vel_model.shape
    chunks = length // ROWS
    tile = (planes, length, lanes)
    tall = (planes, length + 2 * PAD, lanes)
    vmem = pl.BlockSpec(memory_space=pltpu.VMEM)
    anywhere = pl.BlockSpec(memory_space=pl.ANY)
    out = jax.ShapeDtypeStruct((1, *tile), F32)
    return pl.pallas_call(
        functools.partial(kernel, n_shot, n_sub, chunks),
        name="window",
        out_shape=(pltpu.VMEM(out.shape, F32), pltpu.VMEM(out.shape, F32)),
        in_specs=[pl.BlockSpec(memory_space=pltpu.SMEM)] + [vmem] * 4 + [anywhere] * 6,
        out_specs=(vmem, vmem),
        scratch_shapes=[
            *[pltpu.VMEM((2, *tile), BF16) for _ in range(6)],
            pltpu.VMEM(tile, F32),
            pltpu.VMEM(tile, F32),
            pltpu.VMEM(tile, F32),
            pltpu.VMEM((3, *tile), F32),
            pltpu.VMEM((9, *tall), BF16),
            pltpu.VMEM((3, *tall), BF16),
            pltpu.VMEM((9, 2, *tile), BF16),
            pltpu.VMEM((2, *tile), F32),
            pltpu.VMEM((2, *tile), F32),
            pltpu.VMEM((ITERS, *tile), F32),
            pltpu.VMEM((ITERS, 3, *tile), F32),
            pltpu.VMEM(tile, F32),
            pltpu.VMEM((ITERS, *tile), F32),
            pltpu.VMEM(tile, F32),
            pltpu.VMEM(tile, F32),
            pltpu.VMEM((2 * ROWS, PLANES * LANES), F32),
            pltpu.VMEM((PLANES * ROWS, 2 * LANES), F32),
            *[pltpu.VMEM((2, *tile), BF16) for _ in range(6)],
            pltpu.VMEM((2, 2, *tile), BF16),
            pltpu.VMEM((LANES, receivers.shape[1]), BF16),
            pltpu.VMEM((ITERS, LANES, 2 * receivers.shape[1]), BF16),
            pltpu.SemaphoreType.DMA((6,)),
            pltpu.SemaphoreType.DMA((6,)),
            pltpu.SemaphoreType.DMA((chunks, 4)),
            pltpu.SemaphoreType.DMA((9, 2)),
            pltpu.SemaphoreType.DMA((9, chunks)),
            pltpu.SemaphoreType.DMA((2, 6)),
            pltpu.SemaphoreType.DMA((2, chunks, 3)),
        ],
        compiler_params=pltpu.CompilerParams(
            collective_id=0, has_side_effects=True, vmem_limit_bytes=60 * 1024 * 1024
        ),
    )(
        cover, receivers, observed, jnp.asarray(band_y()), jnp.asarray(band_z()),
        vel_model, den_model, p_now, p_before, q_now, q_before,
    )


def solution(mesh):
    tiles = P("shot", "sub", None, None)
    return jax.shard_map(
        body,
        mesh=mesh,
        in_specs=(
            tiles, tiles, P(), P("shot", None), P("shot", None, None), tiles, tiles, tiles, tiles,
        ),
        out_specs=(tiles, tiles),
        check_vma=False,
    )
```

```python
import functools

import jax
import jax.numpy as jnp
import ml_dtypes
import numpy as np
from jax import lax
from jax.experimental import pallas as pl
from jax.experimental.pallas import tpu as pltpu
from jax.sharding import PartitionSpec as P

MESH = pl.DeviceIdType.MESH
BF16 = jnp.bfloat16
F32 = jnp.float32

ITERS = 4
SECOND = (-205.0 / 72.0, 8.0 / 5.0, -1.0 / 5.0, 8.0 / 315.0, -1.0 / 560.0)
FIRST = (4.0 / 5.0, -1.0 / 5.0, 4.0 / 105.0, -1.0 / 280.0)
SECOND_WHOLE = (8064.0, -1008.0, 128.0, -9.0)
FIRST_WHOLE = (672.0, -168.0, 32.0, -3.0)
SPEED = 0.15

PLANES = 4
ROWS = 64
PAD = 16
WINDOW = ROWS + 2 * PAD
LANES = 128
SUB = 16
LOG = 8
DEN, VEL = 0, 1
TILES_DIRECT = 0
SUMS_DIRECT = (1, 0)


def band_y():
    taps = np.zeros((2 * ROWS, 2 * WINDOW), np.float32)
    for row in range(ROWS):
        for m in range(1, 5):
            for base in (0, WINDOW):
                taps[row, base + PAD + row + m] = SECOND_WHOLE[m - 1]
                taps[row, base + PAD + row - m] = SECOND_WHOLE[m - 1]
                taps[ROWS + row, base + PAD + row + m] = FIRST_WHOLE[m - 1]
                taps[ROWS + row, base + PAD + row - m] = -FIRST_WHOLE[m - 1]
    return taps.astype(ml_dtypes.bfloat16)


def band_z():
    taps = np.zeros((2 * LANES, 2 * LANES), np.float32)
    for out in range(LANES):
        for m in range(1, 5):
            for base in (0, LANES):
                if out + m < LANES:
                    taps[base + out + m, out] = SECOND_WHOLE[m - 1]
                    taps[base + out + m, LANES + out] = FIRST_WHOLE[m - 1]
                if out - m >= 0:
                    taps[base + out - m, out] = SECOND_WHOLE[m - 1]
                    taps[base + out - m, LANES + out] = -FIRST_WHOLE[m - 1]
    return taps.astype(ml_dtypes.bfloat16)


def kernel(
    n_shot, n_sub, chunks,
    cover, receivers, observed, taps_y, taps_z,
    vel_hbm, den_hbm, p_now, p_before, q_now, q_before,
    grad_vel, grad_den,
    own_tile, left_tile, right_tile, far_tile, pair_tile, pair_out,
    velocity, density, log_den, slopes, high, low, halo, field, adj,
    kept_l, kept_d, count, source, sum_vel, sum_den, y_part, z_part,
    shot_out, shot_pair, far_out, far_in, right_out, left_out, near_in,
    spot, seen, load_sem, g_send, g_recv, h_send, h_recv, r_send, r_recv,
):
    s = lax.axis_index("shot")
    c = lax.axis_index("sub")
    right = (lax.rem(s + 2, n_shot), c)
    left = (lax.rem(s + n_shot - 2, n_shot), c)
    far = (lax.rem(s + 4, n_shot), c)
    y_hi = lax.rem(s, 2)
    pair = (s + 1 - 2 * y_hi, c)
    after = (s, c + 1)
    before = (s, c - 1)
    has_after = c < n_sub - 1
    has_before = c > 0

    loads = [
        pltpu.make_async_copy(den_hbm.at[0], own_tile.at[DEN], load_sem.at[0]),
        pltpu.make_async_copy(vel_hbm.at[0], own_tile.at[VEL], load_sem.at[1]),
        pltpu.make_async_copy(p_now.at[0], field.at[0], load_sem.at[2]),
        pltpu.make_async_copy(p_before.at[0], field.at[1], load_sem.at[3]),
        pltpu.make_async_copy(q_now.at[0], adj.at[0], load_sem.at[4]),
        pltpu.make_async_copy(q_before.at[0], adj.at[1], load_sem.at[5]),
    ]
    for load in loads:
        load.start()

    barrier = pltpu.get_barrier_semaphore()
    for other in (right, left, far, pair):
        pl.semaphore_signal(barrier, 1, device_id=other, device_id_type=MESH)

    @pl.when(has_after)
    def _():
        pl.semaphore_signal(barrier, 1, device_id=after, device_id_type=MESH)

    @pl.when(has_before)
    def _():
        pl.semaphore_signal(barrier, 1, device_id=before, device_id_type=MESH)

    mine = cover[s, c]
    theirs = cover[pair[0], c]

    def row_of(step):
        return lax.rem(s + 2 * step, n_shot)

    def flag(test):
        return jnp.where(test, 1.0, 0.0).astype(F32)

    steps = (0, 3, 1, 2)
    mine_is = [flag(mine == row_of(k)) for k in steps]
    theirs_is = [flag(theirs == row_of(k)) for k in steps]
    mine_pair = flag(lax.rem(mine, 2) != y_hi)

    def rows(chunk, group=None):
        if group is None:
            return pl.ds(pl.multiple_of(chunk * ROWS, ROWS), ROWS)
        return pl.ds(pl.multiple_of(chunk * ROWS + group * SUB, SUB), SUB)

    def padded(chunk, group=None):
        if group is None:
            return pl.ds(pl.multiple_of(chunk * ROWS + PAD, SUB), ROWS)
        return pl.ds(pl.multiple_of(chunk * ROWS + group * SUB + PAD, SUB), SUB)

    low_half, high_half = pl.ds(0, 2), pl.ds(2, 2)
    every = pl.ds(0, PLANES)

    both = pl.ds(0, 2)
    tiles_relayed = chunks - TILES_DIRECT
    sums_relayed = (chunks - SUMS_DIRECT[DEN], chunks - SUMS_DIRECT[VEL])

    def remote(src, dst, send, recv, to):
        return pltpu.make_async_remote_copy(
            src_ref=src, dst_ref=dst, send_sem=send, recv_sem=recv, device_id=to, device_id_type=MESH
        )

    def g_copy(kind, chunk):
        part = rows(chunk)
        if kind == 0:
            src, dst, to = own_tile.at[both, every, part], left_tile.at[both, every, part], right
        elif kind == 1:
            src, dst, to = own_tile.at[both, every, part], right_tile.at[both, every, part], left
        elif kind == 2:
            src, dst, to = (
                left_tile.at[both, low_half, part], far_tile.at[both, low_half, part], right
            )
        elif kind == 3:
            src, dst, to = (
                right_tile.at[both, high_half, part], far_tile.at[both, high_half, part], left
            )
        elif kind == 4:
            src, dst, to = pair_out.at[both, every, part], pair_tile.at[both, every, part], pair
        else:
            src, dst, to = own_tile.at[both, every, part], far_tile.at[both, every, part], far
        return remote(src, dst, g_send.at[kind], g_recv.at[chunk, (0, 1, 2, 2, 3, 2)[kind]], to)

    def g_wait_far(chunk):
        whole = far_tile.at[both, every, rows(chunk)]
        remote(whole, whole, g_send.at[2], g_recv.at[chunk, 2], right).wait_recv()

    def g_drain():
        for kind in range(6):
            planes = low_half if kind in (2, 3) else every
            sent = {2: tiles_relayed, 3: tiles_relayed, 5: chunks - tiles_relayed}.get(kind, chunks)
            if sent:
                whole = far_tile.at[both, planes, pl.ds(0, sent * ROWS)]
                remote(whole, whole, g_send.at[kind], g_recv.at[0, 0], right).wait_send()

    def h_copy(side, e, chunk):
        return remote(
            high.at[e, every, padded(chunk)], halo.at[e, side, every, rows(chunk)],
            h_send.at[e, side], h_recv.at[e, chunk], after if side == 0 else before,
        )

    def h_start(e, chunk):
        @pl.when(has_after)
        def _():
            h_copy(0, e, chunk).start()

        @pl.when(has_before)
        def _():
            h_copy(1, e, chunk).start()

    inside = jnp.logical_and(has_before, has_after)

    def h_wait_recv(e, chunk):
        @pl.when(inside)
        def _():
            whole = halo.at[e, both, every, rows(chunk)]
            remote(whole, whole, h_send.at[e, 0], h_recv.at[e, chunk], right).wait_recv()

        @pl.when(jnp.logical_not(inside))
        def _():
            one = halo.at[e, 0, every, rows(chunk)]
            remote(one, one, h_send.at[e, 0], h_recv.at[e, chunk], right).wait_recv()

    def h_drain(e, _):
        whole = halo.at[e, 0]

        @pl.when(has_after)
        def _():
            remote(whole, whole, h_send.at[e, 0], h_recv.at[e, 0], right).wait_send()

        @pl.when(has_before)
        def _():
            remote(whole, whole, h_send.at[e, 1], h_recv.at[e, 0], right).wait_send()

        return 0

    def r_copy(kind, b, chunk):
        part = rows(chunk)
        if kind == 0:
            src, dst, to = shot_out.at[b, every, part], shot_pair.at[b, every, part], pair
        elif kind == 1:
            src, dst, to = far_out.at[b, low_half, part], far_in.at[b, low_half, part], right
        elif kind == 2:
            src, dst, to = far_out.at[b, high_half, part], far_in.at[b, high_half, part], left
        elif kind == 3:
            src, dst, to = right_out.at[b, every, part], near_in.at[b, 0, every, part], right
        elif kind == 4:
            src, dst, to = left_out.at[b, every, part], near_in.at[b, 1, every, part], left
        else:
            src, dst, to = far_out.at[b, every, part], far_in.at[b, every, part], far
        return remote(
            src, dst, r_send.at[b, kind], r_recv.at[b, chunk, (0, 1, 1, 2, 2, 1)[kind]], to
        )

    def r_wait_far(b, chunk):
        whole = far_in.at[b, every, rows(chunk)]
        remote(whole, whole, r_send.at[b, 1], r_recv.at[b, chunk, 1], right).wait_recv()

    def r_wait_near(b, chunk):
        whole = near_in.at[b, both, every, rows(chunk)]
        remote(whole, whole, r_send.at[b, 3], r_recv.at[b, chunk, 2], right).wait_recv()

    def r_drain():
        for b in (DEN, VEL):
            for kind in range(6):
                planes = low_half if kind in (1, 2) else every
                relayed = sums_relayed[b]
                sent = {1: relayed, 2: relayed, 5: chunks - relayed}.get(kind, chunks)
                if sent:
                    whole = far_in.at[b, planes, pl.ds(0, sent * ROWS)]
                    remote(whole, whole, r_send.at[b, kind], r_recv.at[0, 0, 0], right).wait_send()

    def put_split(e, slot, chunk, group, value):
        top = value.astype(BF16)
        high[e, :, padded(chunk, group), :] = top
        low[slot, :, padded(chunk, group), :] = (value - top.astype(F32)).astype(BF16)

    def matrix_part(e, slot, chunk):
        window = pl.ds(pl.multiple_of(chunk * ROWS, ROWS), WINDOW)
        columns = jnp.concatenate(
            [
                jnp.concatenate([ref[at_, plane, window, :] for plane in range(PLANES)], axis=1)
                for ref, at_ in ((high, e), (low, slot))
            ],
            axis=0,
        )
        y_part[...] = jnp.dot(taps_y[...], columns, preferred_element_type=F32)
        lines = jnp.concatenate(
            [
                jnp.concatenate(
                    [high[e, plane, padded(chunk), :], low[slot, plane, padded(chunk), :]], axis=1
                )
                for plane in range(PLANES)
            ],
            axis=0,
        )
        z_part[...] = jnp.dot(lines, taps_z[...], preferred_element_type=F32)

    def from_y(group, second):
        part = pl.ds((0 if second else ROWS) + group * SUB, SUB)
        return jnp.stack(
            [y_part[part, pl.ds(plane * LANES, LANES)] for plane in range(PLANES)], axis=0
        )

    def from_z(group, second):
        lanes = pl.ds(0 if second else LANES, LANES)
        return jnp.stack(
            [z_part[pl.ds(plane * ROWS + group * SUB, SUB), lanes] for plane in range(PLANES)],
            axis=0,
        )

    def vector_part(own, e, chunk, group, second):
        wide = jnp.concatenate(
            [
                halo[e, 0, :, rows(chunk, group), :].astype(F32),
                own,
                halo[e, 1, :, rows(chunk, group), :].astype(F32),
            ],
            axis=0,
        )
        d_x = None
        laplace = (3.0 * SECOND[0]) * own if second else None
        for m in range(1, 5):
            up, down = wide[4 + m : 8 + m], wide[4 - m : 8 - m]
            term = FIRST[m - 1] * (up - down)
            d_x = term if d_x is None else d_x + term
            if second:
                laplace = laplace + SECOND[m] * (up + down)
        d_y = from_y(group, False) * (1.0 / 840.0)
        d_z = from_z(group, False) * (1.0 / 840.0)
        if second:
            laplace = laplace + (from_y(group, True) + from_z(group, True)) * (1.0 / 5040.0)
        return laplace, (d_x, d_y, d_z)

    groups = ROWS // SUB

    def operate(laplace, diffs, chunk, group):
        part = rows(chunk, group)
        return laplace - (
            slopes[0, :, part, :] * diffs[0]
            + slopes[1, :, part, :] * diffs[1]
            + slopes[2, :, part, :] * diffs[2]
        )

    def take_tiles(chunk):
        g_copy(0, chunk).start()
        g_copy(1, chunk).start()
        pl.when(chunk >= tiles_relayed)(lambda: g_copy(5, chunk).start())

    def relay_tiles(chunk):
        g_copy(0, chunk).wait_recv()
        pl.when(chunk < tiles_relayed)(lambda: g_copy(2, chunk).start())
        g_copy(1, chunk).wait_recv()
        pl.when(chunk < tiles_relayed)(lambda: g_copy(3, chunk).start())

    def chosen(a, part, flags):
        total = own_tile[a, :, part, :].astype(F32) * flags[0]
        for ref, one in zip((left_tile, right_tile, far_tile), flags[1:]):
            total = total + ref[a, :, part, :].astype(F32) * one
        return total

    def pair_tiles(chunk):
        g_wait_far(chunk)
        for group in range(groups):
            part = rows(chunk, group)
            for a in (DEN, VEL):
                pair_out[a, :, part, :] = chosen(a, part, theirs_is).astype(BF16)
        g_copy(4, chunk).start()

    def finish_density(chunk):
        g_copy(4, chunk).wait_recv()
        for group in range(groups):
            part = rows(chunk, group)
            value = chosen(DEN, part, mine_is) + pair_tile[DEN, :, part, :].astype(F32) * mine_pair
            density[:, part, :] = value
            logs = jnp.log(value)
            log_den[:, part, :] = logs
            put_split(LOG, 2, chunk, group, logs)
        h_start(LOG, chunk)

    def finish_velocity(chunk):
        for group in range(groups):
            part = rows(chunk, group)
            velocity[:, part, :] = (
                chosen(VEL, part, mine_is) + pair_tile[VEL, :, part, :].astype(F32) * mine_pair
            )

    def make_slopes(chunk):
        h_wait_recv(LOG, chunk)
        matrix_part(LOG, 2, chunk)
        for group in range(groups):
            part = rows(chunk, group)
            _, diffs = vector_part(log_den[:, part, :], LOG, chunk, group, False)
            for d in range(3):
                slopes[d, :, part, :] = diffs[d]

    def forward(chunk, n):
        now, other = lax.rem(n, 2), lax.rem(n + 1, 2)
        h_wait_recv(n, chunk)
        matrix_part(n, now, chunk)

        last = n == ITERS - 1
        for group in range(groups):
            part = rows(chunk, group)
            own = field[now, :, part, :]
            laplace, diffs = vector_part(own, n, chunk, group, True)
            applied = operate(laplace, diffs, chunk, group)
            kept_l[n, :, part, :] = applied
            for d in range(3):
                kept_d[n, d, :, part, :] = diffs[d]
            vel = velocity[:, part, :]
            moved = 2.0 * own - field[other, :, part, :] + (SPEED * vel * vel) * applied
            misfit = count[:, part, :] * moved - source[n, :, part, :]
            source[n, :, part, :] = misfit
            following = jnp.where(last, adj[0, :, part, :] + misfit, moved)
            field[other, :, part, :] = following
            put_split(n + 1, other, chunk, group, following)
        h_start(n + 1, chunk)

    def backward(chunk, n):
        now, other = lax.rem(n, 2), lax.rem(n + 1, 2)
        k = n - ITERS
        h_wait_recv(n, chunk)
        matrix_part(n, now, chunk)
        for group in range(groups):
            part = rows(chunk, group)
            own = field[now, :, part, :]
            laplace, diffs = vector_part(own, n, chunk, group, True)
            applied = operate(laplace, diffs, chunk, group)
            vel = velocity[:, part, :]
            moved = 2.0 * own - adj[other, :, part, :] + (SPEED * vel * vel) * applied
            adj[other, :, part, :] = moved
            following = moved + source[2 - k, :, part, :]
            field[other, :, part, :] = following
            put_split(n + 1, other, chunk, group, following)
            total = sum_vel[:, part, :] + own * kept_l[3 - k, :, part, :]
            sum_vel[:, part, :] = total
            sum_den[:, part, :] += (
                diffs[0] * kept_d[3 - k, 0, :, part, :]
                + diffs[1] * kept_d[3 - k, 1, :, part, :]
                + diffs[2] * kept_d[3 - k, 2, :, part, :]
            )

            @pl.when(k == 2)
            def _():
                whole = total + following * kept_l[0, :, part, :]
                shot_out[VEL, :, part, :] = (2.0 * SPEED * vel * whole).astype(BF16)

        h_start(n + 1, chunk)

        @pl.when(k == 2)
        def _():
            r_copy(0, VEL, chunk).start()

    def backward_last(chunk):
        n = 2 * ITERS - 1
        h_wait_recv(n, chunk)
        matrix_part(n, n % 2, chunk)
        for group in range(groups):
            part = rows(chunk, group)
            own = field[n % 2, :, part, :]
            _, diffs = vector_part(own, n, chunk, group, False)
            whole = sum_den[:, part, :] + (
                diffs[0] * kept_d[0, 0, :, part, :]
                + diffs[1] * kept_d[0, 1, :, part, :]
                + diffs[2] * kept_d[0, 2, :, part, :]
            )
            vel = velocity[:, part, :]
            shot_out[DEN, :, part, :] = (
                (SPEED * vel * vel) / density[:, part, :] * whole
            ).astype(BF16)
        r_copy(0, DEN, chunk).start()

    def whole_flag(one):
        return jnp.full((1, SUB, LANES), one, F32).astype(BF16)

    def sent_step(b, part, which):
        return shot_out[b, :, part, :] * whole_flag(mine_is[which]) + shot_pair[
            b, :, part, :
        ] * whole_flag(theirs_is[which])

    def for_step(b, part, which):
        return (
            shot_out[b, :, part, :].astype(F32) * mine_is[which]
            + shot_pair[b, :, part, :].astype(F32) * theirs_is[which]
        )

    def reduce_far(b, chunk):
        r_copy(0, b, chunk).wait_recv()
        straight = chunk >= sums_relayed[b]
        for group in range(groups):
            part = rows(chunk, group)
            far_out[b, :, part, :] = sent_step(b, part, 3)

        @pl.when(straight)
        def _():
            r_copy(5, b, chunk).start()
            for group in range(groups):
                part = rows(chunk, group)
                right_out[b, :, part, :] = sent_step(b, part, 2)
                left_out[b, :, part, :] = sent_step(b, part, 1)
            r_copy(3, b, chunk).start()
            r_copy(4, b, chunk).start()

        @pl.when(jnp.logical_not(straight))
        def _():
            r_copy(1, b, chunk).start()
            r_copy(2, b, chunk).start()

    def reduce_near(b, chunk):
        @pl.when(chunk < sums_relayed[b])
        def _():
            r_wait_far(b, chunk)
            for group in range(groups):
                part = rows(chunk, group)
                arrived = far_in[b, :, part, :]
                to_right = sent_step(b, part, 2)
                to_left = sent_step(b, part, 1)
                right_out[b, 0:2, part, :] = to_right[0:2] + arrived[0:2]
                right_out[b, 2:4, part, :] = to_right[2:4]
                left_out[b, 0:2, part, :] = to_left[0:2]
                left_out[b, 2:4, part, :] = to_left[2:4] + arrived[2:4]
            r_copy(3, b, chunk).start()
            r_copy(4, b, chunk).start()

    def reduce_end(b, chunk):
        r_wait_near(b, chunk)
        out = grad_vel if b == VEL else grad_den
        for group in range(groups):
            part = rows(chunk, group)
            out[0, :, part, :] = (
                for_step(b, part, 0)
                + near_in[b, 0, :, part, :].astype(F32)
                + near_in[b, 1, :, part, :].astype(F32)
            )

        @pl.when(chunk >= sums_relayed[b])
        def _():
            r_wait_far(b, chunk)
            for group in range(groups):
                part = rows(chunk, group)
                out[0, :, part, :] += far_in[b, :, part, :].astype(F32)

    for ref in (high, low):
        edge = jnp.zeros((ref.shape[0], PLANES, PAD, LANES), BF16)
        ref[:, :, 0:PAD, :] = edge
        ref[:, :, PAD + chunks * ROWS :, :] = edge

    def clear_side(side):
        def clear(i, _):
            halo[i, side] = jnp.zeros((PLANES, chunks * ROWS, LANES), BF16)
            return 0

        lax.fori_loop(0, 9, clear, 0)

    pl.when(c == 0)(lambda: clear_side(0))
    pl.when(c == n_sub - 1)(lambda: clear_side(1))

    loads[2].wait()

    def first_field(chunk, _):
        for group in range(groups):
            put_split(0, 0, chunk, group, field[0, :, rows(chunk, group), :])
        return 0

    lax.fori_loop(0, chunks, first_field, 0)

    cells = PLANES * chunks * ROWS * LANES
    n_rec = receivers.shape[1]

    def receiver_lanes():
        lane = (receivers[...] - c * cells) & (LANES - 1)
        at_lane = (lax.broadcasted_iota(jnp.int32, (LANES, n_rec), 0) == lane).astype(F32)
        spot[...] = at_lane.astype(BF16)
        for n in range(ITERS):
            values = at_lane * observed[0, n : n + 1, :]
            top = values.astype(BF16)
            seen[n, :, 0:n_rec] = top
            seen[n, :, n_rec : 2 * n_rec] = (values - top.astype(F32)).astype(BF16)

    contract = (((1,), (1,)), ((), ()))

    def receivers_of_plane(plane):
        line = lax.shift_right_arithmetic(receivers[...] - c * cells, 7)
        lines = lax.broadcasted_iota(jnp.int32, (chunks * ROWS, n_rec), 0) + plane * (chunks * ROWS)
        at_line = (lines == line).astype(F32).astype(BF16)
        count[plane] = lax.dot_general(at_line, spot[...], contract, preferred_element_type=F32)
        twice = jnp.concatenate([at_line, at_line], axis=1)
        for n in range(ITERS):
            source[n, plane] = lax.dot_general(
                twice, seen[n], contract, preferred_element_type=F32
            )

    def clear_sums(plane, _):
        sum_vel[plane] = jnp.zeros((chunks * ROWS, LANES), F32)
        sum_den[plane] = jnp.zeros((chunks * ROWS, LANES), F32)
        return 0

    lax.fori_loop(0, PLANES, clear_sums, 0)
    receiver_lanes()

    loads[0].wait()
    loads[1].wait()
    barrier_count = 4 + has_after.astype(jnp.int32) + has_before.astype(jnp.int32)
    pl.semaphore_wait(barrier, barrier_count)

    for chunk in range(2):
        take_tiles(chunk)

    def first_halo(chunk, _):
        h_start(0, chunk)
        return 0

    lax.fori_loop(0, chunks, first_halo, 0)

    for load in loads[3:]:
        load.wait()

    def at(chunk, event):
        pl.when(jnp.logical_and(chunk >= 0, chunk < chunks))(lambda: event(chunk))

    first_wave = 3
    n_waves = chunks + 2 * ITERS - 1
    ticks = first_wave + n_waves + 4

    def tick(t, _):
        def plane_pair(pair_index):
            receivers_of_plane(2 * pair_index)
            receivers_of_plane(2 * pair_index + 1)

        def finish(chunk):
            finish_density(chunk)
            finish_velocity(chunk)

        at(t, relay_tiles)
        at(t + 2, take_tiles)
        at(t - 1, pair_tiles)
        at(t - 2, finish)
        pl.when(t < 2)(lambda: plane_pair(t))
        wave = t - first_wave
        at(wave, make_slopes)

        def reduce_lag(b, wave_of):
            at(wave - wave_of - 1, functools.partial(reduce_far, b))
            at(wave - wave_of - 2, functools.partial(reduce_near, b))
            at(wave - wave_of - 4, functools.partial(reduce_end, b))

        def process(n, _):
            chunk = wave - n
            pl.when(n < ITERS)(lambda: forward(chunk, n))
            pl.when(jnp.logical_and(n >= ITERS, n < 2 * ITERS - 1))(lambda: backward(chunk, n))
            pl.when(n == 2 * ITERS - 1)(lambda: backward_last(chunk))
            return 0

        lax.fori_loop(
            jnp.maximum(wave - (chunks - 1), 0), jnp.minimum(wave + 1, 2 * ITERS), process, 0
        )
        @pl.when(wave == n_waves)
        def _():
            g_drain()
            lax.fori_loop(0, 9, h_drain, 0)

        reduce_lag(VEL, 6)
        reduce_lag(DEN, 7)
        return 0

    lax.fori_loop(0, ticks, tick, 0)

    r_drain()


def body(vel_model, den_model, cover, receivers, observed, p_now, p_before, q_now, q_before):
    n_shot, n_sub = lax.axis_size("shot"), lax.axis_size("sub")
    _, planes, length, lanes = vel_model.shape
    chunks = length // ROWS
    tile = (planes, length, lanes)
    tall = (planes, length + 2 * PAD, lanes)
    vmem = pl.BlockSpec(memory_space=pltpu.VMEM)
    anywhere = pl.BlockSpec(memory_space=pl.ANY)
    out = jax.ShapeDtypeStruct((1, *tile), F32)
    return pl.pallas_call(
        functools.partial(kernel, n_shot, n_sub, chunks),
        name="window",
        out_shape=(pltpu.VMEM(out.shape, F32), pltpu.VMEM(out.shape, F32)),
        in_specs=[pl.BlockSpec(memory_space=pltpu.SMEM)] + [vmem] * 4 + [anywhere] * 6,
        out_specs=(vmem, vmem),
        scratch_shapes=[
            *[pltpu.VMEM((2, *tile), BF16) for _ in range(6)],
            pltpu.VMEM(tile, F32),
            pltpu.VMEM(tile, F32),
            pltpu.VMEM(tile, F32),
            pltpu.VMEM((3, *tile), F32),
            pltpu.VMEM((9, *tall), BF16),
            pltpu.VMEM((3, *tall), BF16),
            pltpu.VMEM((9, 2, *tile), BF16),
            pltpu.VMEM((2, *tile), F32),
            pltpu.VMEM((2, *tile), F32),
            pltpu.VMEM((ITERS, *tile), F32),
            pltpu.VMEM((ITERS, 3, *tile), F32),
            pltpu.VMEM(tile, F32),
            pltpu.VMEM((ITERS, *tile), F32),
            pltpu.VMEM(tile, F32),
            pltpu.VMEM(tile, F32),
            pltpu.VMEM((2 * ROWS, PLANES * LANES), F32),
            pltpu.VMEM((PLANES * ROWS, 2 * LANES), F32),
            *[pltpu.VMEM((2, *tile), BF16) for _ in range(6)],
            pltpu.VMEM((2, 2, *tile), BF16),
            pltpu.VMEM((LANES, receivers.shape[1]), BF16),
            pltpu.VMEM((ITERS, LANES, 2 * receivers.shape[1]), BF16),
            pltpu.SemaphoreType.DMA((6,)),
            pltpu.SemaphoreType.DMA((6,)),
            pltpu.SemaphoreType.DMA((chunks, 4)),
            pltpu.SemaphoreType.DMA((9, 2)),
            pltpu.SemaphoreType.DMA((9, chunks)),
            pltpu.SemaphoreType.DMA((2, 6)),
            pltpu.SemaphoreType.DMA((2, chunks, 3)),
        ],
        compiler_params=pltpu.CompilerParams(
            collective_id=0, has_side_effects=True, vmem_limit_bytes=60 * 1024 * 1024
        ),
    )(
        cover, receivers, observed, jnp.asarray(band_y()), jnp.asarray(band_z()),
        vel_model, den_model, p_now, p_before, q_now, q_before,
    )


def solution(mesh):
    tiles = P("shot", "sub", None, None)
    return jax.shard_map(
        body,
        mesh=mesh,
        in_specs=(
            tiles, tiles, P(), P("shot", None), P("shot", None, None), tiles, tiles, tiles, tiles,
        ),
        out_specs=(tiles, tiles),
        check_vma=False,
    )
```
